256 devices in a mesh: seq: 16 (over y, z_lo, core), chan: 16 (over z_hi, x).
Axes of the slice: x: 4, y: 4, z: 8 (z_hi: 4, z_lo: 2; z = z_hi * 2 + z_lo), core: 2. Of those that a mesh axis runs over, the one named last changes fastest.
Arguments:
- key_proj: bfloat16 [8192, 4096], P('seq', 'chan'), may hold values from -6 to 6
- value_proj: bfloat16 [8192, 4096], P('seq', 'chan'), may hold values from -6 to 6
- grad_out: bfloat16 [8192, 4096], P('seq', 'chan'), may hold values from -6 to 6
- filter_taps: bfloat16 [8192, 256], P('seq'), may hold values from -0.0625 to 0.0625
- skip_gain: float32 [4096], P('chan'), may hold values from -4 to 4
Outputs:
- key_grad: bfloat16 [8192, 4096], P('seq', 'chan')
- value_grad: bfloat16 [8192, 4096], P('seq', 'chan')
- filter_grad: float32 [8192, 256], P(('seq', 'chan'))
- bias_grad: float32 [4096], P(('chan', 'seq'))
The draws below stay inside these ranges and needn't reach their ends.
All inputs are finite; a program needn't handle non-finite values.
Results may differ from the reference program's by a relative error of at most 0.009.
Values may be sent and summed in bfloat16 or wider, within the bound.
A program may use at most 128 MiB of HBM per device.

```python
import jax
import jax.numpy as jnp
from jax import lax

CHANNELS = 4096
FILTERS = 256
SEQLEN = 8192


def shard_levels(key, shape, split, least, largest):
    def one(position, shards_of):
        heights = jax.random.uniform(jax.random.fold_in(jax.random.fold_in(key, 6), position), (shards_of,), jnp.float32, least / len(split), largest / len(split))
        return jnp.repeat(jnp.exp(heights), shape[position] // shards_of).reshape((-1,) + (1,) * (len(shape) - position - 1))

    loudness = one(*split[0])
    for cut in split[1:]:
        loudness = loudness * one(*cut)
    return loudness


def scatter_about(stream_key, shape, spread, bound, split=(), kind=jnp.bfloat16):
    drawn = spread * jax.random.normal(stream_key, shape, jnp.float32)
    if split:
        drawn = drawn * shard_levels(stream_key, shape, split, -0.22, 0.18)
    return jnp.clip(drawn, -bound, bound).astype(kind)


def setup_inputs(seed: int = 0) -> dict:
    key_list = jax.random.split(jax.random.key(seed), 6)
    return {
        "key_proj": scatter_about(key_list[0], (SEQLEN, CHANNELS), 1.0, 6.0, ((0, 16), (1, 16))),
        "value_proj": scatter_about(key_list[1], (SEQLEN, CHANNELS), 1.0, 6.0, ((0, 16), (1, 16))),
        "grad_out": scatter_about(key_list[2], (SEQLEN, CHANNELS), 1.0, 6.0, ((0, 16), (1, 16))),
        "filter_taps": scatter_about(key_list[3], (SEQLEN, FILTERS), (1.0 / SEQLEN ** 0.5), 0.0625, ((0, 16),)),
        "skip_gain": scatter_about(key_list[4], (CHANNELS,), 1.0, 4.0, ((0, 16),), jnp.float32),
    }


def reference(key_proj, value_proj, grad_out, filter_taps, skip_gain):
    seq_length, chan_count = key_proj.shape
    filter_count = filter_taps.shape[1]
    groups = chan_count // filter_count
    padded = 2 * seq_length
    scale_norm = seq_length ** -0.5
    filter_scale = (seq_length * groups) ** -0.5
    shared = filter_taps.astype(jnp.float32)
    filter_spectrum = jnp.fft.rfft(shared, n=padded, axis=0)

    def regroup(array):
        return array.reshape(seq_length, groups, filter_count).transpose(1, 0, 2)

    def one_group(running, group_data):
        key_block, value_block, grad_block, gain_block = group_data
        key_float = key_block.astype(jnp.float32)
        value_float = value_block.astype(jnp.float32)
        mixed = (key_float * value_float).astype(jnp.bfloat16)
        mixed_float = lax.optimization_barrier(mixed).astype(jnp.float32)
        grad_float = grad_block.astype(jnp.float32)
        mixed_spectrum = jnp.fft.rfft(mixed_float, n=padded, axis=0)
        grad_spectrum = jnp.fft.rfft(grad_float, n=padded, axis=0)
        conv_grad = jnp.fft.irfft(grad_spectrum * jnp.conj(filter_spectrum), n=padded, axis=0)[:seq_length]
        filter_part = jnp.fft.irfft(grad_spectrum * jnp.conj(mixed_spectrum), n=padded, axis=0)[:seq_length]
        mixed_grad = conv_grad + gain_block[None, :] * grad_float
        key_grad = (mixed_grad * value_float).astype(jnp.bfloat16)
        value_grad = (mixed_grad * key_float).astype(jnp.bfloat16)
        bias_part = jnp.sum(grad_float * mixed_float, axis=0) * scale_norm
        return running + filter_part, (key_grad, value_grad, bias_part)

    start_value = jnp.zeros((seq_length, filter_count), jnp.float32)
    filter_sum, outputs = lax.scan(one_group, start_value, (regroup(key_proj), regroup(value_proj), regroup(grad_out), skip_gain.reshape(groups, filter_count)))
    key_grad = outputs[0].transpose(1, 0, 2).reshape(seq_length, chan_count)
    value_grad = outputs[1].transpose(1, 0, 2).reshape(seq_length, chan_count)
    bias_grad = outputs[2].reshape(chan_count)
    filter_grad = filter_sum * filter_scale
    return key_grad, value_grad, filter_grad, bias_grad
```

```python
import functools
import math

import jax
import jax.numpy as jnp
from jax import lax
from jax.experimental import pallas as pl
from jax.experimental.pallas import tpu as pltpu
from jax.sharding import PartitionSpec as P

MESH = pl.DeviceIdType.MESH
F32, BF16 = jnp.float32, jnp.bfloat16
NT = (((1,), (1,)), ((), ()))


def dot_nt(a, b):
    return lax.dot_general(a, b, NT, preferred_element_type=F32)


def iotas(rows, cols=128):
    lane = lax.broadcasted_iota(jnp.int32, (rows, cols), 1)
    return lane, lax.broadcasted_iota(jnp.int32, (rows, cols), 0)


def eye(size):
    lane, row = iotas(size, size)
    return jnp.where(lane == row, 1.0, 0.0).astype(BF16)


def halves(low, high):
    sub = lax.broadcasted_iota(jnp.int32, low.shape, 1)
    return jnp.where(sub < 4, low, high)


def turn(rows):
    return pltpu.roll(rows, 4, 1)


def to_tiles(block, tiles):
    flipped = dot_nt(eye(256), block).reshape(32, 8, 512)
    v = [flipped[:, :, 128 * jj : 128 * jj + 128] for jj in range(4)]
    even = jnp.concatenate([halves(v[0], turn(v[1])), halves(v[2], turn(v[3]))], axis=1)
    odd = jnp.concatenate([halves(turn(v[0]), v[1]), halves(turn(v[2]), v[3])], axis=1)
    tiles[...] = jnp.stack([even, odd], axis=1).reshape(64, 16, 128).astype(BF16)


def from_tiles(tiles):
    pairs = tiles[...].astype(F32).reshape(32, 32, 128)
    e0, e1, o0, o1 = (pairs[:, 8 * i : 8 * i + 8, :] for i in range(4))
    v = [halves(e0, turn(o0)), halves(turn(e0), o0), halves(e1, turn(o1)), halves(turn(e1), o1)]
    return [dot_nt(eye(128), one.reshape(256, 128).astype(BF16)) for one in v]


def unpack_tiles(src, dst, base, count):
    def one(i, c):
        rows = pl.ds(pl.multiple_of(base + 128 * i, 8), 128)
        dst[rows, :] = src[pl.ds(8 * i, 8)].astype(F32).reshape(128, 128)
        return c

    lax.fori_loop(0, count // 8, one, 0)


def build_toeplitz(h32, f, t_ref):
    lane, row = iotas(128)
    mask = lane + row < 128

    def one(e, c):
        rows = [h32[pl.ds(8 + 4 * (8 * e + i - 1) + f, 1), :] for i in range(9)]
        for i in range(8):
            before = jnp.broadcast_to(rows[i], (128, 128))
            here = jnp.broadcast_to(rows[i + 1], (128, 128))
            t = pltpu.roll(jnp.where(mask, here, before), 0, 1, stride=1, stride_axis=0)
            par, d0 = i // 4, i % 4
            t_ref[e, 128 * par : 128 * par + 128, 128 * d0 : 128 * d0 + 128] = t.astype(BF16)
        return c

    lax.fori_loop(0, 8, one, 0)


def build_gcat(g32, f, gcat, gt5):
    jj = lax.broadcasted_iota(jnp.int32, (256, 128), 0) % 4
    unit = eye(128)
    for d0 in range(5):
        block = g32[pl.ds(f + 4 * (d0 if d0 < 4 else 16), 256, stride=4), :]
        if 0 < d0 < 4:
            later = g32[pl.ds(f + 4 * (d0 + 12), 256, stride=4), :]
            block = jnp.where(jj + d0 < 4, block, later)
        block = block.astype(BF16)
        if d0 < 4:
            gcat[:, 128 * d0 : 128 * d0 + 128] = block
        gt5[128 * d0 : 128 * d0 + 128, :] = dot_nt(unit, block).astype(BF16)


def convolve(gcat, t_ref, acc):
    acc[...] = jnp.zeros_like(acc)
    for e in range(8):
        n = 256 - 32 * e
        y = dot_nt(gcat[32 * e : 256, :], t_ref[e])
        acc[0:n, :] += y[:, 0:128]
        acc[0 : n - 16, :] += y[16:, 128:256]


def build_rt(m32, f, mpad, rt):
    mpad[128:384, :] = m32[pl.ds(f, 256, stride=4), :].astype(BF16)
    lane, row = iotas(128)
    flip = jnp.where(lane == (row // 16) * 16 + 15 - row % 16, 1.0, 0.0).astype(BF16)
    for d in range(8):
        t = dot_nt(flip, mpad[128 - 16 * d : 384 - 16 * d, :]).astype(BF16)
        for a in range(8):
            piece = t[16 * a : 16 * a + 16, :]
            rt[16 * d : 16 * d + 16, 256 * a : 256 * a + 256] = piece
            rt[128 + 16 * d : 144 + 16 * d, 256 * a + 128 : 256 * a + 256] = piece[:, 0:128]


def correlate(rt, gt5, out):
    for half in range(2):
        acc = None
        for a in range(8):
            rows = gt5[16 * a + 256 * half : 16 * a + 256 * half + 256, :]
            y = dot_nt(rt[:, 256 * a : 256 * a + 256], rows)
            acc = y if acc is None else acc + y
        out[:, 256 * half : 256 * half + 256] = acc


def sum_diagonals(out, f, c_ref):
    lane, row = iotas(16)
    mask = lane + row >= 15
    after = jnp.zeros((16, 128), F32)
    for d1 in reversed(range(16)):
        for d0 in reversed(range(4)):
            here = out[16 * d1 : 16 * d1 + 16, 128 * d0 : 128 * d0 + 128]
            z = pltpu.roll(jnp.where(mask, here, after), 113, 1, stride=1, stride_axis=0)
            after = here
            c_ref[d0, pl.ds(4 * d1 + f, 1), :] = jnp.sum(z[0:8] + z[8:16], axis=0, keepdims=True)


def kernel(
    scales,
    key_ref,
    value_ref,
    grad_ref,
    taps_ref,
    gain_ref,
    key_out,
    value_out,
    filter_out,
    bias_out,
    g_send,
    m_send,
    h_send,
    b_send,
    g_recv,
    m_recv,
    h_recv,
    b_recv,
    y_send,
    y_recv,
    c_ref,
    c_recv,
    c_sum,
    c_last,
    g32,
    m32,
    h32,
    gcat,
    gt5,
    t_ref,
    acc,
    o32,
    mpad,
    rt,
    out,
    turned,
    sends,
    recvs,
):
    bias_scale, filter_scale = scales
    s, k = lax.axis_index("seq"), lax.axis_index("chan")
    y, c = s // 4, s % 4
    z, x = k // 4, k % 4
    me = 4 * s + x

    def group(i):
        s2 = (y + i // 16) % 4 * 4 + (c + i // 4 % 4) % 4
        x2 = (x + i % 4) % 4
        return (s2, 4 * z + x2), 4 * s2 + x2

    def row(i):
        s2 = (y + i // 4) % 4 * 4 + (c + i % 4) % 4
        return (s2, k), s2

    def column(i):
        z2 = (z + i) % 4
        return (s, 4 * z2 + x), z2

    def copy(src, dst, sem, device):
        return pltpu.make_async_remote_copy(
            src_ref=src,
            dst_ref=dst,
            send_sem=sends.at[sem],
            recv_sem=recvs.at[sem],
            device_id=device,
            device_id_type=MESH,
        )

    def all_of(src, dst, sem, count):
        return copy(src.at[pl.ds(0, count)], dst.at[pl.ds(0, count)], sem, group(1)[0])

    def each(lo, hi, body):
        lax.fori_loop(lo, hi, lambda i, none: (body(i), none)[1], 0)

    barrier = pltpu.get_barrier_semaphore()

    def greet(device):
        pl.semaphore_signal(barrier, inc=1, device_id=device, device_id_type=MESH)

    each(1, 64, lambda i: greet(group(i)[0]))
    each(1, 4, lambda i: greet(column(i)[0]))

    to_tiles(taps_ref[...], h_send)
    to_tiles(grad_ref[...], g_send)
    mixed = (key_ref[...].astype(F32) * value_ref[...].astype(F32)).astype(BF16)
    to_tiles(mixed, m_send)
    bias_part = jnp.sum(grad_ref[...].astype(F32) * mixed.astype(F32), axis=0, keepdims=True)
    b_send[...] = jnp.broadcast_to(bias_part, (8, 256))

    pl.semaphore_wait(barrier, 66)

    def send_taps(i):
        device, s2 = row(i)
        copy(h_send.at[4 * s2 + x], h_recv.at[s], 0, device).start()

    def send_grad(i):
        device, other = group(i)
        copy(g_send.at[other], g_recv.at[me], 1, device).start()

    def send_mixed(i):
        device, other = group(i)
        copy(m_send.at[other], m_recv.at[me], 2, device).start()

    def send_bias(i):
        device, s2 = row(i)
        copy(b_send, b_recv.at[s], 3, device).start()

    each(1, 16, send_taps)
    each(1, 64, send_grad)
    each(1, 64, send_mixed)
    each(1, 16, send_bias)
    h_recv[s] = h_send[me]
    g_recv[me] = g_send[me]
    m_recv[me] = m_send[me]
    b_recv[s] = b_send[...]

    h32[0:8, :] = jnp.zeros((8, 128), F32)
    g32[1024:1088, :] = jnp.zeros((64, 128), F32)
    mpad[0:128, :] = jnp.zeros((128, 128), BF16)
    rt[...] = jnp.zeros_like(rt)

    all_of(h_send, h_recv, 0, 15).wait()
    unpack_tiles(h_recv, h32, 8, 16)
    each(0, 4, lambda f: build_toeplitz(h32, f, t_ref.at[f]))

    all_of(g_send, g_recv, 1, 63).wait()
    unpack_tiles(g_recv, g32, 0, 64)

    def one_conv(f):
        build_gcat(g32, f, gcat, gt5.at[f])
        convolve(gcat, t_ref.at[f], acc)
        o32[pl.ds(f, 256, stride=4), :] = acc[...]

    each(0, 4, one_conv)

    def pack(i):
        rows = pl.ds(pl.multiple_of(128 * i, 8), 128)
        y_send[pl.ds(8 * i, 8)] = o32[rows, :].reshape(8, 16, 128).astype(BF16)

    each(0, 8, pack)

    def send_conv(i):
        device, other = group(i)
        copy(y_send.at[other], y_recv.at[me], 4, device).start()

    each(1, 64, send_conv)
    y_recv[me] = y_send[me]

    all_of(m_send, m_recv, 2, 63).wait()
    unpack_tiles(m_recv, m32, 0, 64)

    def one_cross(f):
        build_rt(m32, f, mpad, rt)
        correlate(rt, gt5.at[f], out)
        sum_diagonals(out, f, c_ref)

    each(0, 4, one_cross)

    def send_part(i):
        device, z2 = column(i)
        copy(c_ref.at[z2], c_recv.at[z], 5, device).start()

    each(1, 4, send_part)
    c_recv[z] = c_ref[z]
    all_of(c_ref, c_recv, 5, 3).wait()
    total = c_recv[0] + c_recv[1] + c_recv[2] + c_recv[3]
    c_sum[...] = (total * filter_scale).reshape(8, 8, 128)

    def send_cross(i):
        device, other = group(i)
        copy(c_sum.at[other // 8], c_last.at[me], 6, device).start()

    each(1, 64, send_cross)
    c_last[me] = c_sum[s // 2]

    all_of(y_send, y_recv, 4, 63).wait()
    conv = from_tiles(y_recv)
    for jj in range(4):
        rows = slice(128 * jj, 128 * jj + 128)
        mixed_grad = conv[jj] + gain_ref[...] * grad_ref[rows, :].astype(F32)
        key_out[rows, :] = (mixed_grad * value_ref[rows, :].astype(F32)).astype(BF16)
        value_out[rows, :] = (mixed_grad * key_ref[rows, :].astype(F32)).astype(BF16)

    copy(b_recv.at[pl.ds(0, 15)], b_recv.at[pl.ds(0, 15)], 3, group(1)[0]).wait()
    bias = jnp.sum(b_recv[...], axis=0) * bias_scale
    bias_out[...] = pltpu.roll(bias, (256 - 16 * s) % 256, 1)[0:1, 0:16]

    copy(c_last.at[pl.ds(0, 63)], c_last.at[pl.ds(0, 63)], 6, group(1)[0]).wait()
    parts = c_last[...]
    parts = jnp.where(s % 2 == 0, parts, turn(parts)).reshape(32, 2, 8, 128)
    rows = halves(parts[:, 0], turn(parts[:, 1])).reshape(256, 128)
    turned[...] = rows.T
    filter_out[...] = turned[pl.ds(pl.multiple_of(32 * x, 32), 32), :]


def per_device(scales, key_proj, value_proj, grad_out, filter_taps, skip_gain):
    vmem = pl.BlockSpec(memory_space=pltpu.VMEM)
    tiles = pltpu.VMEM((64, 16, 128), BF16)
    outs = pl.pallas_call(
        functools.partial(kernel, scales),
        out_shape=(
            jax.ShapeDtypeStruct((512, 256), BF16),
            jax.ShapeDtypeStruct((512, 256), BF16),
            jax.ShapeDtypeStruct((32, 256), F32),
            jax.ShapeDtypeStruct((1, 16), F32),
        ),
        in_specs=[vmem] * 5,
        out_specs=(vmem,) * 4,
        scratch_shapes=[
            tiles,
            tiles,
            tiles,
            pltpu.VMEM((8, 256), F32),
            tiles,
            tiles,
            pltpu.VMEM((16, 16, 128), BF16),
            pltpu.VMEM((16, 8, 256), F32),
            tiles,
            tiles,
            pltpu.VMEM((4, 64, 128), F32),
            pltpu.VMEM((4, 64, 128), F32),
            pltpu.VMEM((8, 8, 128), F32),
            pltpu.VMEM((64, 8, 128), F32),
            pltpu.VMEM((1088, 128), F32),
            pltpu.VMEM((1024, 128), F32),
            pltpu.VMEM((264, 128), F32),
            pltpu.VMEM((256, 512), BF16),
            pltpu.VMEM((4, 640, 256), BF16),
            pltpu.VMEM((4, 8, 256, 512), BF16),
            pltpu.VMEM((256, 128), F32),
            pltpu.VMEM((1024, 128), F32),
            pltpu.VMEM((384, 128), BF16),
            pltpu.VMEM((256, 2048), BF16),
            pltpu.VMEM((256, 512), F32),
            pltpu.VMEM((128, 256), F32),
            pltpu.SemaphoreType.DMA((7,)),
            pltpu.SemaphoreType.DMA((7,)),
        ],
        name="hyena_backward",
        compiler_params=pltpu.CompilerParams(
            collective_id=0, has_side_effects=True, vmem_limit_bytes=48 << 20
        ),
    )(key_proj, value_proj, grad_out, filter_taps, skip_gain.reshape(1, 256))
    return outs[0], outs[1], outs[2], outs[3].reshape(16)


def solution(mesh):
    in_specs = (P("seq", "chan"), P("seq", "chan"), P("seq", "chan"), P("seq", None), P("chan"))
    out_specs = (P("seq", "chan"), P("seq", "chan"), P(("seq", "chan"), None), P(("chan", "seq")))
    scales = (1.0 / math.sqrt(8192), 1.0 / math.sqrt(8192 * 16))
    return jax.shard_map(
        functools.partial(per_device, scales),
        mesh=mesh,
        in_specs=in_specs,
        out_specs=out_specs,
        check_vma=False,
    )
```

```python
import functools
import math

import jax
import jax.numpy as jnp
from jax import lax
from jax.experimental import pallas as pl
from jax.experimental.pallas import tpu as pltpu
from jax.sharding import PartitionSpec as P

MESH = pl.DeviceIdType.MESH
F32, BF16 = jnp.float32, jnp.bfloat16
NT = (((1,), (1,)), ((), ()))


def dot_nt(a, b):
    return lax.dot_general(a, b, NT, preferred_element_type=F32)


def iotas(rows, cols=128):
    lane = lax.broadcasted_iota(jnp.int32, (rows, cols), 1)
    return lane, lax.broadcasted_iota(jnp.int32, (rows, cols), 0)


def eye(size):
    lane, row = iotas(size, size)
    return jnp.where(lane == row, 1.0, 0.0).astype(BF16)


def halves(low, high):
    sub = lax.broadcasted_iota(jnp.int32, low.shape, 1)
    return jnp.where(sub < 4, low, high)


def turn(rows):
    return pltpu.roll(rows, 4, 1)


def to_tiles(block, tiles):
    flipped = dot_nt(eye(256), block).reshape(32, 8, 512)
    v = [flipped[:, :, 128 * jj : 128 * jj + 128] for jj in range(4)]
    even = jnp.concatenate([halves(v[0], turn(v[1])), halves(v[2], turn(v[3]))], axis=1)
    odd = jnp.concatenate([halves(turn(v[0]), v[1]), halves(turn(v[2]), v[3])], axis=1)
    tiles[...] = jnp.stack([even, odd], axis=1).reshape(64, 16, 128).astype(BF16)


def pair_rows(block):
    flipped = dot_nt(eye(256), block).reshape(32, 8, 512)
    sub = lax.broadcasted_iota(jnp.int32, (32, 8, 128), 1) // 2
    turned = [[pltpu.roll(flipped[:, :, 128 * jj : 128 * jj + 128], 2 * r, 1) if r else flipped[:, :, 128 * jj : 128 * jj + 128] for r in range(4)] for jj in range(4)]

    def merge(shift):
        rows = turned[0][-shift % 4]
        for jj in range(1, 4):
            rows = jnp.where(sub == jj, turned[jj][(jj - shift) % 4], rows)
        return rows

    return [[merge(2 * par + hf) for par in range(2)] for hf in range(2)]


def to_pair_tiles(grad, mixed, tiles):
    g, m = pair_rows(grad), pair_rows(mixed)
    for hf in range(2):
        both = [jnp.concatenate([g[hf][par], m[hf][par]], axis=1) for par in range(2)]
        tiles[hf] = jnp.stack(both, axis=1).reshape(64, 16, 128).astype(BF16)


def from_tiles(tiles):
    pairs = tiles[...].astype(F32).reshape(32, 32, 128)
    e0, e1, o0, o1 = (pairs[:, 8 * i : 8 * i + 8, :] for i in range(4))
    v = [halves(e0, turn(o0)), halves(turn(e0), o0), halves(e1, turn(o1)), halves(turn(e1), o1)]
    return [dot_nt(eye(128), one.reshape(256, 128).astype(BF16)) for one in v]


def unpack_taps(src, dst):
    for i in range(2):
        dst[8 + 128 * i : 136 + 128 * i, :] = src[8 * i : 8 * i + 8].astype(F32).reshape(128, 128)


def unpack_pairs(src, g32, m32):
    def one(i, c):
        rows = pl.ds(pl.multiple_of(128 * i, 128), 128)
        both = src[pl.ds(16 * i, 16)].astype(F32)
        g32[rows, :] = both[:, 0:8, :].reshape(128, 128)
        m32[rows, :] = both[:, 8:16, :].reshape(128, 128)
        return c

    lax.fori_loop(0, 4, one, 0)


def build_toeplitz(h32, f, t_ref, i):
    lane, row = iotas(128)
    mask = lane + row < 128
    e, par = i // 2, i % 2
    rows = [h32[pl.ds(8 + 4 * (4 * i + j - 1) + f, 1), :] for j in range(5)]
    for d0 in range(4):
        before = jnp.broadcast_to(rows[d0], (128, 128))
        here = jnp.broadcast_to(rows[d0 + 1], (128, 128))
        t = pltpu.roll(jnp.where(mask, here, before), 0, 1, stride=1, stride_axis=0)
        t_ref[e, 128 * par : 128 * par + 128, 128 * d0 : 128 * d0 + 128] = t.astype(BF16)


def build_gcat(g32, f, gcat, gt5):
    jj = lax.broadcasted_iota(jnp.int32, (256, 128), 0) % 4
    unit = eye(128)
    for d0 in range(5):
        block = g32[pl.ds(f + 2 * (d0 if d0 < 4 else 16), 256, stride=2), :]
        if 0 < d0 < 4:
            later = g32[pl.ds(f + 2 * (d0 + 12), 256, stride=2), :]
            block = jnp.where(jj + d0 < 4, block, later)
        block = block.astype(BF16)
        if d0 < 4:
            gcat[:, 128 * d0 : 128 * d0 + 128] = block
        gt5[128 * d0 : 128 * d0 + 128, :] = dot_nt(unit, block).astype(BF16)


def convolve(gcat, t_ref, acc):
    acc[...] = jnp.zeros_like(acc)
    for e in range(8):
        n = 256 - 32 * e
        y = dot_nt(gcat[32 * e : 256, :], t_ref[e])
        acc[0:n, :] += y[:, 0:128]
        acc[0 : n - 16, :] += y[16:, 128:256]


def build_rt(m32, f, mpad, rt):
    mpad[128:384, :] = m32[pl.ds(f, 256, stride=2), :].astype(BF16)
    lane, row = iotas(128)
    flip = jnp.where(lane == (row // 16) * 16 + 15 - row % 16, 1.0, 0.0).astype(BF16)
    for d in range(8):
        t = dot_nt(flip, mpad[128 - 16 * d : 384 - 16 * d, :]).astype(BF16)
        for a in range(8):
            piece = t[16 * a : 16 * a + 16, :]
            rt[16 * d : 16 * d + 16, 256 * a : 256 * a + 256] = piece
            rt[128 + 16 * d : 144 + 16 * d, 256 * a + 128 : 256 * a + 256] = piece[:, 0:128]


def correlate(rt, gt5, out, beside):
    for half in range(2):
        acc = None
        for a in range(8):
            rows = gt5[16 * a + 256 * half : 16 * a + 256 * half + 256, :]
            y = dot_nt(rt[:, 256 * a : 256 * a + 256], rows)
            acc = y if acc is None else acc + y
            beside(8 * half + a)
        out[:, 256 * half : 256 * half + 256] = acc


def sum_diagonals(out, f, c_ref):
    lane, row = iotas(16)
    mask = lane + row >= 15
    after = jnp.zeros((16, 128), F32)
    for d1 in reversed(range(16)):
        for d0 in reversed(range(4)):
            here = out[16 * d1 : 16 * d1 + 16, 128 * d0 : 128 * d0 + 128]
            z = pltpu.roll(jnp.where(mask, here, after), 113, 1, stride=1, stride_axis=0)
            after = here
            c_ref[d0, pl.ds(4 * d1 + f, 1), :] = jnp.sum(z[0:8] + z[8:16], axis=0, keepdims=True)


def sum_bias(g32, m32, b_send):
    parts = []
    for hf in range(2):

        def one(i, sums):
            rows = pl.ds(pl.multiple_of(32 * i, 32), 32)
            return sums + g32[hf, rows, :] * m32[hf, rows, :]

        sums = lax.fori_loop(0, 16, one, jnp.zeros((32, 128), F32)).reshape(4, 8, 128)
        sums = sums + turn(sums)
        parts.append(sums + pltpu.roll(sums, 2, 1))
    sub = lax.broadcasted_iota(jnp.int32, (4, 8, 128), 1)
    b_send[...] = jnp.where(sub // 2 % 2 == 0, parts[0], parts[1])


def kernel(
    filter_scale,
    key_ref,
    value_ref,
    grad_ref,
    taps_ref,
    y_recv,
    c_last,
    b_recv,
    key_in,
    value_in,
    grad_in,
    taps_in,
    h_send,
    h_recv,
    x_send,
    x_recv,
    b_send,
    y_send,
    c_ref,
    c_recv,
    c_sum,
    g32,
    m32,
    h32,
    gcat,
    gt5,
    t_ref,
    acc,
    o32,
    mpad,
    rt,
    out,
    loads,
    sends,
    recvs,
):
    s, k = lax.axis_index("seq"), lax.axis_index("chan")
    y, c = s // 4, s % 4
    z, x = k // 4, k % 4
    me = 4 * s + x

    def group(i):
        s2 = (y + i // 16) % 4 * 4 + (c + i // 4 % 4) % 4
        x2 = (x + i % 4) % 4
        return (s2, 4 * z + x2), 4 * s2 + x2

    def row(i):
        s2 = (y + i // 4) % 4 * 4 + (c + i % 4) % 4
        return (s2, k), s2

    def column(i):
        z2 = (z + i) % 4
        return (s, 4 * z2 + x), z2

    def copy(src, dst, sem, device):
        return pltpu.make_async_remote_copy(
            src_ref=src,
            dst_ref=dst,
            send_sem=sends.at[sem],
            recv_sem=recvs.at[sem],
            device_id=device,
            device_id_type=MESH,
        )

    def all_of(src, dst, sem, count):
        return copy(src.at[pl.ds(0, count)], dst.at[pl.ds(0, count)], sem, group(1)[0])

    def each(lo, hi, body):
        lax.fori_loop(lo, hi, lambda i, none: (body(i), none)[1], 0)

    def others(count, body):
        for i in reversed(range(1, count)):
            body(i)

    inputs = ((taps_ref, taps_in), (grad_ref, grad_in), (key_ref, key_in), (value_ref, value_in))
    fetches = [pltpu.make_async_copy(src, dst, loads.at[i]) for i, (src, dst) in enumerate(inputs)]
    for fetch in fetches:
        fetch.start()

    barrier = pltpu.get_barrier_semaphore()

    def greet(device):
        pl.semaphore_signal(barrier, inc=1, device_id=device, device_id_type=MESH)

    others(64, lambda i: greet(group(i)[0]))
    others(4, lambda i: greet(column(i)[0]))

    fetches[0].wait()
    to_tiles(taps_in[...], h_send)
    for fetch in fetches[1:]:
        fetch.wait()
    mixed = (key_in[...].astype(F32) * value_in[...].astype(F32)).astype(BF16)
    to_pair_tiles(grad_in[...], mixed, x_send)

    h32[0:8, :] = jnp.zeros((8, 128), F32)
    for hf in range(2):
        g32[hf, 512:544, :] = jnp.zeros((32, 128), F32)
    mpad[0:128, :] = jnp.zeros((128, 128), BF16)
    rt[...] = jnp.zeros_like(rt)

    pl.semaphore_wait(barrier, 66)

    def send_taps(i):
        device, s2 = row(i)
        copy(h_send.at[4 * s2 + x], h_recv.at[s], 0, device).start()

    def send_pairs(hf):
        def send(i):
            device, other = group(i)
            copy(x_send.at[hf, other], x_recv.at[hf, me], 1 + hf, device).start()

        return send

    others(16, send_taps)
    others(64, send_pairs(0))
    others(64, send_pairs(1))
    h_recv[s] = h_send[me]
    for hf in range(2):
        x_recv[hf, me] = x_send[hf, me]

    all_of(h_send, h_recv, 0, 15).wait()
    unpack_taps(h_recv, h32)

    for hf in range(2):
        all_of(x_send.at[hf], x_recv.at[hf], 1 + hf, 63).wait()
        unpack_pairs(x_recv.at[hf], g32.at[hf], m32.at[hf])

        def one_cross(f2):
            f = 2 * hf + f2
            build_gcat(g32.at[hf], f2, gcat.at[f], gt5)
            build_rt(m32.at[hf], f2, mpad, rt)
            correlate(rt, gt5, out, lambda i: build_toeplitz(h32, f, t_ref.at[f], i))
            sum_diagonals(out, f, c_ref)

        each(0, 2, one_cross)

    def send_part(i):
        device, z2 = column(i)
        copy(c_ref.at[z2], c_recv.at[z], 3, device).start()

    others(4, send_part)
    c_recv[z] = c_ref[z]

    sum_bias(g32, m32, b_send)

    def send_bias(i):
        x2 = (x + i) % 4
        copy(b_send.at[x2], b_recv.at[x], 4, (s, 4 * z + x2)).start()

    others(4, send_bias)

    def one_conv(f):
        convolve(gcat.at[f], t_ref.at[f], acc)
        o32[pl.ds(f, 256, stride=4), :] = acc[...]

    each(0, 4, one_conv)

    def pack(i):
        rows = pl.ds(pl.multiple_of(128 * i, 8), 128)
        y_send[pl.ds(8 * i, 8)] = o32[rows, :].reshape(8, 16, 128).astype(BF16)

    each(0, 8, pack)

    def send_conv(i):
        device, other = group(i)
        copy(y_send.at[other], y_recv.at[me], 5, device).start()

    others(64, send_conv)

    all_of(c_ref, c_recv, 3, 3).wait()
    total = c_recv[0] + c_recv[1] + c_recv[2] + c_recv[3]
    c_sum[...] = (total * filter_scale).reshape(16, 4, 128)

    def send_cross(i):
        device, other = group(i)
        copy(c_sum.at[other // 4], c_last.at[me], 6, device).start()

    others(64, send_cross)
    mine = [
        pltpu.make_async_copy(b_send.at[x], b_recv.at[x], loads.at[0]),
        pltpu.make_async_copy(y_send.at[me], y_recv.at[me], loads.at[1]),
        pltpu.make_async_copy(c_sum.at[s], c_last.at[me], loads.at[2]),
    ]
    for one in mine:
        one.start()
    for one in mine:
        one.wait()

    all_of(b_send, b_recv, 4, 3).wait()
    all_of(y_send, y_recv, 5, 63).wait()
    copy(c_last.at[pl.ds(0, 63)], c_last.at[pl.ds(0, 63)], 6, group(1)[0]).wait()


def finish(
    bias_scale,
    key_ref,
    value_ref,
    grad_ref,
    y_ref,
    c_ref,
    b_ref,
    gain_ref,
    key_out,
    value_out,
    filter_out,
    bias_out,
    key_in,
    value_in,
    grad_in,
    y_in,
    c_in,
    b_in,
    key_grad,
    value_grad,
    turned,
    bias_grad,
    loads,
    stores,
):
    x = lax.axis_index("chan") % 4
    inputs = (
        (y_ref, y_in),
        (grad_ref, grad_in),
        (value_ref, value_in),
        (key_ref, key_in),
        (c_ref, c_in),
        (b_ref, b_in),
    )
    fetches = [pltpu.make_async_copy(src, dst, loads.at[i]) for i, (src, dst) in enumerate(inputs)]
    for fetch in fetches:
        fetch.start()
    started = []

    def store(src, dst):
        started.append(pltpu.make_async_copy(src, dst, stores.at[len(started)]))
        started[-1].start()

    for fetch in fetches[:4]:
        fetch.wait()
    conv = from_tiles(y_in)
    for jj in range(4):
        rows = slice(128 * jj, 128 * jj + 128)
        mixed_grad = conv[jj] + gain_ref[...] * grad_in[rows, :].astype(F32)
        key_grad[rows, :] = (mixed_grad * value_in[rows, :].astype(F32)).astype(BF16)
        value_grad[rows, :] = (mixed_grad * key_in[rows, :].astype(F32)).astype(BF16)
    store(key_grad, key_out)
    store(value_grad, value_out)
    fetches[4].wait()
    turned[...] = c_in[...].reshape(256, 128).T
    store(turned.at[pl.ds(pl.multiple_of(32 * x, 32), 32), :], filter_out)
    fetches[5].wait()
    sums = b_in[...]
    sub = lax.broadcasted_iota(jnp.int32, (8, 128), 0)
    sums = jnp.concatenate([jnp.where(sub < 4, sums[0], sums[1]), jnp.where(sub < 4, sums[2], sums[3])], axis=0)
    bias_grad[...] = jnp.sum(sums.T, axis=0, keepdims=True) * bias_scale
    store(bias_grad, bias_out)
    for one in started:
        one.wait()


def per_device(scales, key_proj, value_proj, grad_out, filter_taps, skip_gain):
    bias_scale, filter_scale = scales
    vmem = pl.BlockSpec(memory_space=pltpu.VMEM)
    hbm = pl.BlockSpec(memory_space=pltpu.HBM)
    block = jax.ShapeDtypeStruct((512, 256), BF16)
    outs = pl.pallas_call(
        functools.partial(kernel, filter_scale),
        out_shape=(
            jax.ShapeDtypeStruct((64, 16, 128), BF16),
            jax.ShapeDtypeStruct((64, 4, 128), F32),
            jax.ShapeDtypeStruct((4, 8, 128), F32),
        ),
        in_specs=[hbm] * 4,
        out_specs=(hbm,) * 3,
        scratch_shapes=[
            pltpu.VMEM((512, 256), BF16),
            pltpu.VMEM((512, 256), BF16),
            pltpu.VMEM((512, 256), BF16),
            pltpu.VMEM((512, 256), BF16),
            pltpu.VMEM((64, 16, 128), BF16),
            pltpu.VMEM((16, 16, 128), BF16),
            pltpu.VMEM((2, 64, 16, 128), BF16),
            pltpu.VMEM((2, 64, 16, 128), BF16),
            pltpu.VMEM((4, 8, 128), F32),
            pltpu.VMEM((64, 16, 128), BF16),
            pltpu.VMEM((4, 64, 128), F32),
            pltpu.VMEM((4, 64, 128), F32),
            pltpu.VMEM((16, 4, 128), F32),
            pltpu.VMEM((2, 544, 128), F32),
            pltpu.VMEM((2, 512, 128), F32),
            pltpu.VMEM((264, 128), F32),
            pltpu.VMEM((4, 256, 512), BF16),
            pltpu.VMEM((640, 256), BF16),
            pltpu.VMEM((4, 8, 256, 512), BF16),
            pltpu.VMEM((256, 128), F32),
            pltpu.VMEM((1024, 128), F32),
            pltpu.VMEM((384, 128), BF16),
            pltpu.VMEM((256, 2048), BF16),
            pltpu.VMEM((256, 512), F32),
            pltpu.SemaphoreType.DMA((4,)),
            pltpu.SemaphoreType.DMA((7,)),
            pltpu.SemaphoreType.DMA((7,)),
        ],
        name="hyena_exchange",
        compiler_params=pltpu.CompilerParams(
            collective_id=0, has_side_effects=True, vmem_limit_bytes=60 << 20
        ),
    )(key_proj, value_proj, grad_out, filter_taps)
    key_grad, value_grad, filter_grad, bias_grad = pl.pallas_call(
        functools.partial(finish, bias_scale),
        out_shape=(
            block,
            block,
            jax.ShapeDtypeStruct((32, 256), F32),
            jax.ShapeDtypeStruct((1, 16), F32),
        ),
        in_specs=[hbm] * 6 + [vmem],
        out_specs=(hbm,) * 4,
        scratch_shapes=[
            pltpu.VMEM((512, 256), BF16),
            pltpu.VMEM((512, 256), BF16),
            pltpu.VMEM((512, 256), BF16),
            pltpu.VMEM((64, 16, 128), BF16),
            pltpu.VMEM((64, 4, 128), F32),
            pltpu.VMEM((4, 8, 128), F32),
            pltpu.VMEM((512, 256), BF16),
            pltpu.VMEM((512, 256), BF16),
            pltpu.VMEM((128, 256), F32),
            pltpu.VMEM((1, 16), F32),
            pltpu.SemaphoreType.DMA((6,)),
            pltpu.SemaphoreType.DMA((4,)),
        ],
        name="hyena_finish",
        compiler_params=pltpu.CompilerParams(vmem_limit_bytes=60 << 20),
    )(key_proj, value_proj, grad_out, *outs, skip_gain.reshape(1, 256))
    return key_grad, value_grad, filter_grad, bias_grad.reshape(16)


def solution(mesh):
    in_specs = (P("seq", "chan"), P("seq", "chan"), P("seq", "chan"), P("seq", None), P("chan"))
    out_specs = (P("seq", "chan"), P("seq", "chan"), P(("seq", "chan"), None), P(("chan", "seq")))
    scales = (1.0 / math.sqrt(8192), 1.0 / math.sqrt(8192 * 16))
    return jax.shard_map(
        functools.partial(per_device, scales),
        mesh=mesh,
        in_specs=in_specs,
        out_specs=out_specs,
        check_vma=False,
    )
```

```python
import functools
import math

import jax
import jax.numpy as jnp
from jax import lax
from jax.experimental import pallas as pl
from jax.experimental.pallas import tpu as pltpu
from jax.sharding import PartitionSpec as P

MESH = pl.DeviceIdType.MESH
F32, BF16 = jnp.float32, jnp.bfloat16
NT = (((1,), (1,)), ((), ()))


def dot_nt(a, b):
    return lax.dot_general(a, b, NT, preferred_element_type=F32)


def iotas(rows, cols=128):
    lane = lax.broadcasted_iota(jnp.int32, (rows, cols), 1)
    return lane, lax.broadcasted_iota(jnp.int32, (rows, cols), 0)


def eye(size):
    lane, row = iotas(size, size)
    return jnp.where(lane == row, 1.0, 0.0).astype(BF16)


def halves(low, high):
    sub = lax.broadcasted_iota(jnp.int32, low.shape, 1)
    return jnp.where(sub < 4, low, high)


def turn(rows):
    return pltpu.roll(rows, 4, 1)


def to_tiles(block, tiles):
    flipped = dot_nt(eye(256), block).reshape(32, 8, 512)
    v = [flipped[:, :, 128 * jj : 128 * jj + 128] for jj in range(4)]
    even = jnp.concatenate([halves(v[0], turn(v[1])), halves(v[2], turn(v[3]))], axis=1)
    odd = jnp.concatenate([halves(turn(v[0]), v[1]), halves(turn(v[2]), v[3])], axis=1)
    tiles[...] = jnp.stack([even, odd], axis=1).reshape(64, 16, 128).astype(BF16)


def pair_rows(block):
    flipped = dot_nt(eye(256), block).reshape(32, 8, 512)
    sub = lax.broadcasted_iota(jnp.int32, (32, 8, 128), 1) // 2
    turned = [[pltpu.roll(flipped[:, :, 128 * jj : 128 * jj + 128], 2 * r, 1) if r else flipped[:, :, 128 * jj : 128 * jj + 128] for r in range(4)] for jj in range(4)]

    def merge(shift):
        rows = turned[0][-shift % 4]
        for jj in range(1, 4):
            rows = jnp.where(sub == jj, turned[jj][(jj - shift) % 4], rows)
        return rows

    return [[merge(2 * par + hf) for par in range(2)] for hf in range(2)]


def to_pair_tiles(grad, mixed, tiles):
    g, m = pair_rows(grad), pair_rows(mixed)
    for hf in range(2):
        both = [jnp.concatenate([g[hf][par], m[hf][par]], axis=1) for par in range(2)]
        tiles[hf] = jnp.stack(both, axis=1).reshape(64, 16, 128).astype(BF16)


def from_tiles(tiles):
    pairs = tiles[...].astype(F32).reshape(32, 32, 128)
    e0, e1, o0, o1 = (pairs[:, 8 * i : 8 * i + 8, :] for i in range(4))
    v = [halves(e0, turn(o0)), halves(turn(e0), o0), halves(e1, turn(o1)), halves(turn(e1), o1)]
    return [dot_nt(eye(128), one.reshape(256, 128).astype(BF16)) for one in v]


def unpack_taps(src, dst):
    lane, row = iotas(128)
    reverse = jnp.where(lane + row == 127, 1.0, 0.0).astype(BF16)
    dst[8:264, :] = jnp.dot(src[...].reshape(256, 128), reverse, preferred_element_type=F32)


def unpack_pairs(src, g32, m32):
    def one(i, c):
        rows = pl.ds(pl.multiple_of(128 * i, 128), 128)
        both = src[pl.ds(16 * i, 16)].astype(F32)
        g32[rows, :] = both[:, 0:8, :].reshape(128, 128)
        m32[rows, :] = both[:, 8:16, :].reshape(128, 128)
        return c

    lax.fori_loop(0, 4, one, 0)


def build_toeplitz(h32, f, t_ref, i):
    lane, row = iotas(128)
    mask = lane + row >= 127
    e, par = i // 2, i % 2
    rows = [h32[pl.ds(8 + 4 * (4 * i + j - 1) + f, 1), :] for j in range(5)]
    for d0 in range(4):
        before = jnp.broadcast_to(rows[d0], (128, 128))
        here = jnp.broadcast_to(rows[d0 + 1], (128, 128))
        t = pltpu.roll(jnp.where(mask, here, before), 1, 1, stride=1, stride_axis=0)
        t_ref[e, 128 * d0 : 128 * d0 + 128, 128 * par : 128 * par + 128] = t.astype(BF16)


def build_gcat(g32, f, gcat, gt5):
    jj = lax.broadcasted_iota(jnp.int32, (256, 128), 0) % 4
    unit = eye(128)
    for d0 in range(5):
        block = g32[pl.ds(f + 2 * (d0 if d0 < 4 else 16), 256, stride=2), :]
        if 0 < d0 < 4:
            later = g32[pl.ds(f + 2 * (d0 + 12), 256, stride=2), :]
            block = jnp.where(jj + d0 < 4, block, later)
        block = block.astype(BF16)
        if d0 < 4:
            gcat[:, 128 * d0 : 128 * d0 + 128] = block
        gt5[128 * d0 : 128 * d0 + 128, :] = dot_nt(unit, block).astype(BF16)


def convolve(gcat, t_ref, acc):
    acc[...] = jnp.zeros_like(acc)
    for e in range(8):
        n = 256 - 32 * e
        y = jnp.dot(gcat[32 * e : 256, :], t_ref[e], preferred_element_type=F32)
        acc[0:n, :] += y[:, 0:128]
        acc[0 : n - 16, :] += y[16:, 128:256]


def build_rt(m32, f, mpad, rt):
    mpad[128:384, :] = m32[pl.ds(f, 256, stride=2), :].astype(BF16)
    lane, row = iotas(128)
    flip = jnp.where(lane == (row // 16) * 16 + 15 - row % 16, 1.0, 0.0).astype(BF16)
    for d in range(8):
        t = dot_nt(flip, mpad[128 - 16 * d : 384 - 16 * d, :]).astype(BF16)
        for a in range(8):
            piece = t[16 * a : 16 * a + 16, :]
            rt[16 * d : 16 * d + 16, 256 * a : 256 * a + 256] = piece
            rt[128 + 16 * d : 144 + 16 * d, 256 * a + 128 : 256 * a + 256] = piece[:, 0:128]


def correlate(rt, gt5, out, beside):
    for half in range(2):
        acc = None
        for a in range(8):
            rows = gt5[16 * a + 256 * half : 16 * a + 256 * half + 256, :]
            y = dot_nt(rt[:, 256 * a : 256 * a + 256], rows)
            acc = y if acc is None else acc + y
            beside(8 * half + a)
        out[:, 256 * half : 256 * half + 256] = acc


def sum_diagonals(out, f2, c_ref):
    lane, row = iotas(16)
    mask = lane + row >= 15
    after = jnp.zeros((16, 128), F32)
    for d1 in reversed(range(16)):
        for d0 in reversed(range(4)):
            here = out[16 * d1 : 16 * d1 + 16, 128 * d0 : 128 * d0 + 128]
            z = pltpu.roll(jnp.where(mask, here, after), 113, 1, stride=1, stride_axis=0)
            after = here
            c_ref[d0, pl.ds(2 * d1 + f2, 1), :] = jnp.sum(z[0:8] + z[8:16], axis=0, keepdims=True)


def sum_bias(g32, m32, b_send):
    parts = []
    for hf in range(2):

        def one(i, sums):
            rows = pl.ds(pl.multiple_of(32 * i, 32), 32)
            return sums + g32[hf, rows, :] * m32[hf, rows, :]

        sums = lax.fori_loop(0, 16, one, jnp.zeros((32, 128), F32)).reshape(4, 8, 128)
        sums = sums + turn(sums)
        parts.append(sums + pltpu.roll(sums, 2, 1))
    sub = lax.broadcasted_iota(jnp.int32, (4, 8, 128), 1)
    b_send[...] = jnp.where(sub // 2 % 2 == 0, parts[0], parts[1])


def regroup(rows):
    lane, row = iotas(64)
    to = row % 4
    result = rows
    for step in range(1, 4):
        moved = jnp.where(to + step < 4, pltpu.roll(rows, 64 - step, 0), pltpu.roll(rows, 4 - step, 0))
        moved = pltpu.roll(moved, 32 * step, 1)
        result = jnp.where((lane // 32 - to + 4) % 4 == step, moved, result)
    return result


def kernel(
    filter_scale,
    key_ref,
    value_ref,
    grad_ref,
    taps_ref,
    gain_ref,
    key_out,
    value_out,
    c_last,
    b_recv,
    y_recv,
    key_grad,
    value_grad,
    key_in,
    value_in,
    grad_in,
    taps_in,
    gain_in,
    h_send,
    h_recv,
    x_send,
    x_recv,
    b_send,
    y_send,
    c_ref,
    c_send,
    c_recv,
    c_sum,
    c_mine,
    g32,
    m32,
    h32,
    gcat,
    gt5,
    t_ref,
    acc,
    o32,
    mpad,
    rt,
    out,
    loads,
    sends,
    recvs,
):
    s, k = lax.axis_index("seq"), lax.axis_index("chan")
    y, c = s // 4, s % 4
    z, x = k // 4, k % 4
    me = 4 * s + x

    def group(i):
        s2 = (y + i // 16) % 4 * 4 + (c + i // 4 % 4) % 4
        x2 = (x + i % 4) % 4
        return (s2, 4 * z + x2), 4 * s2 + x2

    def row(i):
        s2 = (y + i // 4) % 4 * 4 + (c + i % 4) % 4
        return (s2, k), s2

    def column(i):
        z2 = (z + i) % 4
        return (s, 4 * z2 + x), z2

    def copy(src, dst, sem, device):
        return pltpu.make_async_remote_copy(
            src_ref=src,
            dst_ref=dst,
            send_sem=sends.at[sem],
            recv_sem=recvs.at[sem],
            device_id=device,
            device_id_type=MESH,
        )

    def all_of(src, dst, sem, count):
        return copy(src.at[pl.ds(0, count)], dst.at[pl.ds(0, count)], sem, group(1)[0])

    def each(lo, hi, body):
        lax.fori_loop(lo, hi, lambda i, none: (body(i), none)[1], 0)

    def others(count, body):
        for i in reversed(range(1, count)):
            body(i)

    inputs = (
        (taps_ref, taps_in),
        (grad_ref, grad_in),
        (key_ref, key_in),
        (value_ref, value_in),
        (gain_ref, gain_in),
    )
    fetches = [pltpu.make_async_copy(src, dst, loads.at[i]) for i, (src, dst) in enumerate(inputs)]
    for fetch in fetches:
        fetch.start()

    barrier = pltpu.get_barrier_semaphore()

    def greet(device):
        pl.semaphore_signal(barrier, inc=1, device_id=device, device_id_type=MESH)

    others(64, lambda i: greet(group(i)[0]))
    others(4, lambda i: greet(column(i)[0]))

    fetches[0].wait()
    to_tiles(taps_in[...], h_send)
    for fetch in fetches[1:]:
        fetch.wait()
    mixed = (key_in[...].astype(F32) * value_in[...].astype(F32)).astype(BF16)
    to_pair_tiles(grad_in[...], mixed, x_send)

    h32[0:8, :] = jnp.zeros((8, 128), F32)
    for hf in range(2):
        g32[hf, 512:544, :] = jnp.zeros((32, 128), F32)
    mpad[0:128, :] = jnp.zeros((128, 128), BF16)
    rt[...] = jnp.zeros_like(rt)

    pl.semaphore_wait(barrier, 66)

    def send_taps(i):
        device, s2 = row(i)
        copy(h_send.at[4 * s2 + x], h_recv.at[s], 0, device).start()

    def send_pairs(hf):
        def send(i):
            device, other = group(i)
            copy(x_send.at[hf, other], x_recv.at[hf, me], 1 + hf, device).start()

        return send

    others(16, send_taps)
    others(64, send_pairs(0))
    others(64, send_pairs(1))
    h_recv[s] = h_send[me]
    for hf in range(2):
        x_recv[hf, me] = x_send[hf, me]

    all_of(h_send, h_recv, 0, 15).wait()
    unpack_taps(h_recv, h32)

    for hf in range(2):
        all_of(x_send.at[hf], x_recv.at[hf], 1 + hf, 63).wait()
        unpack_pairs(x_recv.at[hf], g32.at[hf], m32.at[hf])

        def one_cross(f2):
            f = 2 * hf + f2
            build_gcat(g32.at[hf], f2, gcat.at[f], gt5)
            build_rt(m32.at[hf], f2, mpad, rt)
            correlate(rt, gt5, out, lambda i: build_toeplitz(h32, f, t_ref.at[f], i))
            sum_diagonals(out, f2, c_ref)

        each(0, 2, one_cross)
        c_send[hf] = c_ref[...].astype(BF16)

        def send_part(i):
            device, z2 = column(i)
            copy(c_send.at[hf, z2], c_recv.at[hf, z], 3 + hf, device).start()

        others(4, send_part)
        c_recv[hf, z] = c_send[hf, z]

    sum_bias(g32, m32, b_send)

    def send_bias(i):
        x2 = (x + i) % 4
        copy(b_send.at[x2], b_recv.at[x], 5, (s, 4 * z + x2)).start()

    others(4, send_bias)

    def one_conv(f):
        convolve(gcat.at[f], t_ref.at[f], acc)
        o32[pl.ds(f, 256, stride=4), :] = acc[...]

    each(0, 4, one_conv)

    def pack(i):
        rows = pl.ds(pl.multiple_of(128 * i, 8), 128)
        y_send[pl.ds(8 * i, 8)] = o32[rows, :].reshape(8, 16, 128).astype(BF16)

    each(0, 8, pack)

    def send_conv(i):
        device, other = group(i)
        copy(y_send.at[other], y_recv.at[me], 6, device).start()

    others(64, send_conv)

    for hf in range(2):
        all_of(c_send.at[hf], c_recv.at[hf], 3 + hf, 3).wait()
        total = jnp.sum(c_recv[hf].astype(F32), axis=0) * filter_scale
        c_sum[:, 2 * hf : 2 * hf + 2, :] = total.reshape(16, 2, 128)
    c_mine[...] = regroup(c_sum[...].reshape(64, 128)).reshape(64, 1, 128)

    def send_cross(i):
        device, other = group(i)
        copy(c_mine.at[other], c_last.at[me], 7, device).start()

    others(64, send_cross)
    y_recv[me] = y_send[me]
    mine = [
        pltpu.make_async_copy(b_send.at[x], b_recv.at[x], loads.at[0]),
        pltpu.make_async_copy(c_mine.at[me], c_last.at[me], loads.at[1]),
        pltpu.make_async_copy(key_grad, key_out, loads.at[2]),
        pltpu.make_async_copy(value_grad, value_out, loads.at[3]),
    ]
    mine[0].start()
    mine[1].start()

    all_of(y_send, y_recv, 6, 63).wait()
    conv = from_tiles(y_recv)
    for jj in range(4):
        rows = slice(128 * jj, 128 * jj + 128)
        mixed_grad = conv[jj] + gain_in[...] * grad_in[rows, :].astype(F32)
        key_grad[rows, :] = (mixed_grad * value_in[rows, :].astype(F32)).astype(BF16)
        value_grad[rows, :] = (mixed_grad * key_in[rows, :].astype(F32)).astype(BF16)
    mine[2].start()
    mine[3].start()

    all_of(b_send, b_recv, 5, 3).wait()
    copy(c_last.at[pl.ds(0, 63)], c_last.at[pl.ds(0, 63)], 7, group(1)[0]).wait()
    for one in mine:
        one.wait()


def spread(parts):
    lane, row = iotas(64, 256)
    total = None
    for f in range(4):
        place = jnp.where(lane == 4 * row + f, 1.0, 0.0).astype(F32)
        moved = jnp.dot(
            parts[32 * f : 32 * f + 32, :], place, precision=lax.Precision.HIGHEST, preferred_element_type=F32
        )
        total = moved if total is None else total + moved
    return total


def finish(
    bias_scale,
    key_ref,
    value_ref,
    c_ref,
    b_ref,
    key_out,
    value_out,
    filter_out,
    bias_out,
    c_in,
    b_in,
    key_in,
    value_in,
    turned,
    bias_grad,
    loads,
    stores,
):
    loaded = [
        pltpu.make_async_copy(c_ref, c_in, loads.at[0]),
        pltpu.make_async_copy(b_ref, b_in, loads.at[1]),
        pltpu.make_async_copy(key_ref, key_in, loads.at[2]),
        pltpu.make_async_copy(value_ref, value_in, loads.at[3]),
    ]
    stored = [
        pltpu.make_async_copy(key_in, key_out, stores.at[0]),
        pltpu.make_async_copy(value_in, value_out, stores.at[1]),
        pltpu.make_async_copy(turned, filter_out, stores.at[2]),
        pltpu.make_async_copy(bias_grad, bias_out, stores.at[3]),
    ]
    for one in loaded:
        one.start()
    loaded[0].wait()
    turned[...] = spread(c_in[...].reshape(64, 128).T)
    stored[2].start()
    loaded[1].wait()
    sums = b_in[...]
    sub = lax.broadcasted_iota(jnp.int32, (8, 128), 0)
    sums = jnp.concatenate([jnp.where(sub < 4, sums[0], sums[1]), jnp.where(sub < 4, sums[2], sums[3])], axis=0)
    bias_grad[...] = jnp.sum(sums.T, axis=0, keepdims=True) * bias_scale
    stored[3].start()
    for load, store in zip(loaded[2:], stored):
        load.wait()
        store.start()
    for one in stored:
        one.wait()


def per_device(scales, key_proj, value_proj, grad_out, filter_taps, skip_gain):
    bias_scale, filter_scale = scales
    hbm = pl.BlockSpec(memory_space=pltpu.HBM)
    block = jax.ShapeDtypeStruct((512, 256), BF16)
    outs = pl.pallas_call(
        functools.partial(kernel, filter_scale),
        out_shape=(
            block,
            block,
            jax.ShapeDtypeStruct((64, 1, 128), F32),
            jax.ShapeDtypeStruct((4, 8, 128), F32),
        ),
        in_specs=[hbm] * 5,
        out_specs=(hbm,) * 4,
        scratch_shapes=[
            pltpu.VMEM((64, 16, 128), BF16),
            pltpu.VMEM((512, 256), BF16),
            pltpu.VMEM((512, 256), BF16),
            pltpu.VMEM((512, 256), BF16),
            pltpu.VMEM((512, 256), BF16),
            pltpu.VMEM((512, 256), BF16),
            pltpu.VMEM((512, 256), BF16),
            pltpu.VMEM((1, 256), F32),
            pltpu.VMEM((64, 16, 128), BF16),
            pltpu.VMEM((16, 16, 128), BF16),
            pltpu.VMEM((2, 64, 16, 128), BF16),
            pltpu.VMEM((2, 64, 16, 128), BF16),
            pltpu.VMEM((4, 8, 128), F32),
            pltpu.VMEM((64, 16, 128), BF16),
            pltpu.VMEM((4, 32, 128), F32),
            pltpu.VMEM((2, 4, 32, 128), BF16),
            pltpu.VMEM((2, 4, 32, 128), BF16),
            pltpu.VMEM((16, 4, 128), F32),
            pltpu.VMEM((64, 1, 128), F32),
            pltpu.VMEM((2, 544, 128), F32),
            pltpu.VMEM((2, 512, 128), F32),
            pltpu.VMEM((264, 128), F32),
            pltpu.VMEM((4, 256, 512), BF16),
            pltpu.VMEM((640, 256), BF16),
            pltpu.VMEM((4, 8, 512, 256), BF16),
            pltpu.VMEM((256, 128), F32),
            pltpu.VMEM((1024, 128), F32),
            pltpu.VMEM((384, 128), BF16),
            pltpu.VMEM((256, 2048), BF16),
            pltpu.VMEM((256, 512), F32),
            pltpu.SemaphoreType.DMA((5,)),
            pltpu.SemaphoreType.DMA((8,)),
            pltpu.SemaphoreType.DMA((8,)),
        ],
        name="hyena_exchange",
        compiler_params=pltpu.CompilerParams(
            collective_id=0, has_side_effects=True, vmem_limit_bytes=60 << 20
        ),
    )(key_proj, value_proj, grad_out, filter_taps, skip_gain.reshape(1, 256))
    key_grad, value_grad, filter_grad, bias_grad = pl.pallas_call(
        functools.partial(finish, bias_scale),
        out_shape=(
            block,
            block,
            jax.ShapeDtypeStruct((32, 256), F32),
            jax.ShapeDtypeStruct((1, 16), F32),
        ),
        in_specs=[hbm] * 4,
        out_specs=(hbm,) * 4,
        scratch_shapes=[
            pltpu.VMEM((64, 1, 128), F32),
            pltpu.VMEM((4, 8, 128), F32),
            pltpu.VMEM((512, 256), BF16),
            pltpu.VMEM((512, 256), BF16),
            pltpu.VMEM((32, 256), F32),
            pltpu.VMEM((1, 16), F32),
            pltpu.SemaphoreType.DMA((4,)),
            pltpu.SemaphoreType.DMA((4,)),
        ],
        name="hyena_finish",
        compiler_params=pltpu.CompilerParams(vmem_limit_bytes=60 << 20),
    )(*outs)
    return key_grad, value_grad, filter_grad, bias_grad.reshape(16)


def solution(mesh):
    in_specs = (P("seq", "chan"), P("seq", "chan"), P("seq", "chan"), P("seq", None), P("chan"))
    out_specs = (P("seq", "chan"), P("seq", "chan"), P(("seq", "chan"), None), P(("chan", "seq")))
    scales = (1.0 / math.sqrt(8192), 1.0 / math.sqrt(8192 * 16))
    return jax.shard_map(
        functools.partial(per_device, scales),
        mesh=mesh,
        in_specs=in_specs,
        out_specs=out_specs,
        check_vma=False,
    )
```

```python
import functools
import math

import jax
import jax.numpy as jnp
from jax import lax
from jax.experimental import pallas as pl
from jax.experimental.pallas import tpu as pltpu
from jax.sharding import PartitionSpec as P

MESH = pl.DeviceIdType.MESH
F32, BF16 = jnp.float32, jnp.bfloat16
NT = (((1,), (1,)), ((), ()))


def farthest_first(count):
    def ring(step):
        return min(step, 4 - step)

    def hops(i):
        if count == 4:
            return ring(i)
        x = i % 4 if count == 64 else 0
        rest = i // 4 if count == 64 else i
        return ring(rest // 4) + rest // 2 % 2 + ring(x)

    return sorted(range(1, count), key=hops, reverse=True)


def dot_nt(a, b):
    return lax.dot_general(a, b, NT, preferred_element_type=F32)


def iotas(rows, cols=128):
    lane = lax.broadcasted_iota(jnp.int32, (rows, cols), 1)
    return lane, lax.broadcasted_iota(jnp.int32, (rows, cols), 0)


def eye(size):
    lane, row = iotas(size, size)
    return jnp.where(lane == row, 1.0, 0.0).astype(BF16)


def halves(low, high):
    sub = lax.broadcasted_iota(jnp.int32, low.shape, 1)
    return jnp.where(sub < 4, low, high)


def turn(rows):
    return pltpu.roll(rows, 4, 1)


def to_tiles(block, tiles):
    flipped = dot_nt(eye(256), block).reshape(32, 8, 512)
    v = [flipped[:, :, 128 * jj : 128 * jj + 128] for jj in range(4)]
    even = jnp.concatenate([halves(v[0], turn(v[1])), halves(v[2], turn(v[3]))], axis=1)
    odd = jnp.concatenate([halves(turn(v[0]), v[1]), halves(turn(v[2]), v[3])], axis=1)
    tiles[...] = jnp.stack([even, odd], axis=1).reshape(64, 16, 128).astype(BF16)


def pair_rows(block):
    flipped = dot_nt(eye(256), block).reshape(32, 8, 512)
    sub = lax.broadcasted_iota(jnp.int32, (32, 8, 128), 1) // 2
    turned = [[pltpu.roll(flipped[:, :, 128 * jj : 128 * jj + 128], 2 * r, 1) if r else flipped[:, :, 128 * jj : 128 * jj + 128] for r in range(4)] for jj in range(4)]

    def merge(shift):
        rows = turned[0][-shift % 4]
        for jj in range(1, 4):
            rows = jnp.where(sub == jj, turned[jj][(jj - shift) % 4], rows)
        return rows

    return [[merge(2 * par + hf) for par in range(2)] for hf in range(2)]


def to_pair_tiles(grad, mixed, tiles):
    g, m = pair_rows(grad), pair_rows(mixed)
    for hf in range(2):
        both = [jnp.concatenate([g[hf][par], m[hf][par]], axis=1) for par in range(2)]
        tiles[hf] = jnp.stack(both, axis=1).reshape(64, 16, 128).astype(BF16)


def from_tiles(tiles):
    pairs = tiles[...].astype(F32).reshape(32, 32, 128)
    e0, e1, o0, o1 = (pairs[:, 8 * i : 8 * i + 8, :] for i in range(4))
    v = [halves(e0, turn(o0)), halves(turn(e0), o0), halves(e1, turn(o1)), halves(turn(e1), o1)]
    return [dot_nt(eye(128), one.reshape(256, 128).astype(BF16)) for one in v]


def unpack_taps(src, dst):
    lane, row = iotas(128)
    reverse = jnp.where(lane + row == 127, 1.0, 0.0).astype(BF16)
    dst[8:264, :] = jnp.dot(src[...].reshape(256, 128), reverse, preferred_element_type=F32)


def unpack_pairs(src, g32, m32):
    def one(i, c):
        rows = pl.ds(pl.multiple_of(128 * i, 128), 128)
        both = src[pl.ds(16 * i, 16)].astype(F32)
        g32[rows, :] = both[:, 0:8, :].reshape(128, 128)
        m32[rows, :] = both[:, 8:16, :].reshape(128, 128)
        return c

    lax.fori_loop(0, 4, one, 0)


def build_toeplitz(h32, f, t_ref, i):
    lane, row = iotas(128)
    mask = lane + row >= 127
    e, par = i // 2, i % 2
    rows = [h32[pl.ds(8 + 4 * (4 * i + j - 1) + f, 1), :] for j in range(5)]
    for d0 in range(4):
        before = jnp.broadcast_to(rows[d0], (128, 128))
        here = jnp.broadcast_to(rows[d0 + 1], (128, 128))
        t = pltpu.roll(jnp.where(mask, here, before), 1, 1, stride=1, stride_axis=0)
        t_ref[e, 128 * d0 : 128 * d0 + 128, 128 * par : 128 * par + 128] = t.astype(BF16)


def build_gcat(g32, f, gcat, gt5):
    jj = lax.broadcasted_iota(jnp.int32, (256, 128), 0) % 4
    unit = eye(128)
    for d0 in range(5):
        block = g32[pl.ds(f + 2 * (d0 if d0 < 4 else 16), 256, stride=2), :]
        if 0 < d0 < 4:
            later = g32[pl.ds(f + 2 * (d0 + 12), 256, stride=2), :]
            block = jnp.where(jj + d0 < 4, block, later)
        block = block.astype(BF16)
        if d0 < 4:
            gcat[:, 128 * d0 : 128 * d0 + 128] = block
        gt5[128 * d0 : 128 * d0 + 128, :] = dot_nt(unit, block).astype(BF16)


def convolve(gcat, t_ref, acc):
    acc[...] = jnp.zeros_like(acc)
    for e in range(8):
        n = 256 - 32 * e
        y = jnp.dot(gcat[32 * e : 256, :], t_ref[e], preferred_element_type=F32)
        acc[0:n, :] += y[:, 0:128]
        acc[0 : n - 16, :] += y[16:, 128:256]


def build_rt(m32, f, mpad, rt):
    mpad[128:384, :] = m32[pl.ds(f, 256, stride=2), :].astype(BF16)
    lane, row = iotas(128)
    flip = jnp.where(lane == (row // 16) * 16 + 15 - row % 16, 1.0, 0.0).astype(BF16)
    for d in range(8):
        t = dot_nt(flip, mpad[128 - 16 * d : 384 - 16 * d, :]).astype(BF16)
        for a in range(8):
            piece = t[16 * a : 16 * a + 16, :]
            rt[16 * d : 16 * d + 16, 256 * a : 256 * a + 256] = piece
            rt[128 + 16 * d : 144 + 16 * d, 256 * a + 128 : 256 * a + 256] = piece[:, 0:128]


def correlate(rt, gt5, out, beside):
    for half in range(2):
        acc = None
        for a in range(8):
            rows = gt5[16 * a + 256 * half : 16 * a + 256 * half + 256, :]
            y = dot_nt(rt[:, 256 * a : 256 * a + 256], rows)
            acc = y if acc is None else acc + y
            beside(8 * half + a)
        out[:, 256 * half : 256 * half + 256] = acc


def sum_diagonals(out, f2, c_ref):
    lane, row = iotas(16)
    mask = lane + row >= 15
    after = jnp.zeros((16, 128), F32)
    for d1 in reversed(range(16)):
        for d0 in reversed(range(4)):
            here = out[16 * d1 : 16 * d1 + 16, 128 * d0 : 128 * d0 + 128]
            z = pltpu.roll(jnp.where(mask, here, after), 113, 1, stride=1, stride_axis=0)
            after = here
            c_ref[d0, pl.ds(2 * d1 + f2, 1), :] = jnp.sum(z[0:8] + z[8:16], axis=0, keepdims=True)


def sum_bias(g32, m32, b_send):
    parts = []
    for hf in range(2):

        def one(i, sums):
            rows = pl.ds(pl.multiple_of(32 * i, 32), 32)
            return sums + g32[hf, rows, :] * m32[hf, rows, :]

        sums = lax.fori_loop(0, 16, one, jnp.zeros((32, 128), F32)).reshape(4, 8, 128)
        sums = sums + turn(sums)
        parts.append(sums + pltpu.roll(sums, 2, 1))
    sub = lax.broadcasted_iota(jnp.int32, (4, 8, 128), 1)
    b_send[...] = jnp.where(sub // 2 % 2 == 0, parts[0], parts[1])


def regroup(rows):
    lane, row = iotas(64)
    to = row % 4
    result = rows
    for step in range(1, 4):
        moved = jnp.where(to + step < 4, pltpu.roll(rows, 64 - step, 0), pltpu.roll(rows, 4 - step, 0))
        moved = pltpu.roll(moved, 32 * step, 1)
        result = jnp.where((lane // 32 - to + 4) % 4 == step, moved, result)
    return result


def kernel(
    filter_scale,
    key_ref,
    value_ref,
    grad_ref,
    taps_ref,
    gain_ref,
    key_out,
    value_out,
    c_last,
    b_recv,
    y_recv,
    key_grad,
    value_grad,
    key_in,
    value_in,
    grad_in,
    taps_in,
    gain_in,
    h_send,
    h_recv,
    x_send,
    x_recv,
    b_send,
    y_send,
    c_ref,
    c_send,
    c_recv,
    c_sum,
    c_mine,
    g32,
    m32,
    h32,
    gcat,
    gt5,
    t_ref,
    acc,
    o32,
    mpad,
    rt,
    out,
    loads,
    sends,
    recvs,
):
    s, k = lax.axis_index("seq"), lax.axis_index("chan")
    y, c = s // 4, s % 4
    z, x = k // 4, k % 4
    me = 4 * s + x

    def group(i):
        s2 = (y + i // 16) % 4 * 4 + (c + i // 4 % 4) % 4
        x2 = (x + i % 4) % 4
        return (s2, 4 * z + x2), 4 * s2 + x2

    def row(i):
        s2 = (y + i // 4) % 4 * 4 + (c + i % 4) % 4
        return (s2, k), s2

    def column(i):
        z2 = (z + i) % 4
        return (s, 4 * z2 + x), z2

    def copy(src, dst, sem, device):
        return pltpu.make_async_remote_copy(
            src_ref=src,
            dst_ref=dst,
            send_sem=sends.at[sem],
            recv_sem=recvs.at[sem],
            device_id=device,
            device_id_type=MESH,
        )

    def all_of(src, dst, sem, count):
        return copy(src.at[pl.ds(0, count)], dst.at[pl.ds(0, count)], sem, group(1)[0])

    def each(lo, hi, body):
        lax.fori_loop(lo, hi, lambda i, none: (body(i), none)[1], 0)

    def others(count, body):
        for i in farthest_first(count):
            body(i)

    inputs = (
        (taps_ref, taps_in),
        (grad_ref, grad_in),
        (key_ref, key_in),
        (value_ref, value_in),
        (gain_ref, gain_in),
    )
    fetches = [pltpu.make_async_copy(src, dst, loads.at[i]) for i, (src, dst) in enumerate(inputs)]
    for fetch in fetches:
        fetch.start()

    barrier = pltpu.get_barrier_semaphore()

    def greet(device):
        pl.semaphore_signal(barrier, inc=1, device_id=device, device_id_type=MESH)

    others(64, lambda i: greet(group(i)[0]))
    others(4, lambda i: greet(column(i)[0]))

    fetches[0].wait()
    to_tiles(taps_in[...], h_send)
    for fetch in fetches[1:]:
        fetch.wait()
    mixed = (key_in[...].astype(F32) * value_in[...].astype(F32)).astype(BF16)
    to_pair_tiles(grad_in[...], mixed, x_send)

    h32[0:8, :] = jnp.zeros((8, 128), F32)
    for hf in range(2):
        g32[hf, 512:544, :] = jnp.zeros((32, 128), F32)
    for f2 in range(2):
        mpad[f2, 0:128, :] = jnp.zeros((128, 128), BF16)
    rt[...] = jnp.zeros_like(rt)

    pl.semaphore_wait(barrier, 66)

    def send_taps(i):
        device, s2 = row(i)
        copy(h_send.at[4 * s2 + x], h_recv.at[s], 0, device).start()

    def send_pairs(hf):
        def send(i):
            device, other = group(i)
            copy(x_send.at[hf, other], x_recv.at[hf, me], 1 + hf, device).start()

        return send

    others(16, send_taps)
    others(64, send_pairs(0))
    others(64, send_pairs(1))
    h_recv[s] = h_send[me]
    for hf in range(2):
        x_recv[hf, me] = x_send[hf, me]

    all_of(h_send, h_recv, 0, 15).wait()
    unpack_taps(h_recv, h32)

    for hf in range(2):
        all_of(x_send.at[hf], x_recv.at[hf], 1 + hf, 63).wait()
        unpack_pairs(x_recv.at[hf], g32.at[hf], m32.at[hf])

        for f2 in range(2):
            f = 2 * hf + f2
            build_gcat(g32.at[hf], f2, gcat.at[f], gt5.at[f2])
            build_rt(m32.at[hf], f2, mpad.at[f2], rt.at[f2])
            correlate(rt.at[f2], gt5.at[f2], out.at[f2], functools.partial(build_toeplitz, h32, f, t_ref.at[f]))
            sum_diagonals(out.at[f2], f2, c_ref)

        c_send[hf] = c_ref[...].astype(BF16)

        def send_part(i):
            device, z2 = column(i)
            copy(c_send.at[hf, z2], c_recv.at[hf, z], 3 + hf, device).start()

        others(4, send_part)
        c_recv[hf, z] = c_send[hf, z]

    def one_conv(f):
        convolve(gcat.at[f], t_ref.at[f], acc)
        o32[pl.ds(f, 256, stride=4), :] = acc[...]

    each(0, 4, one_conv)

    def pack(i):
        rows = pl.ds(pl.multiple_of(128 * i, 8), 128)
        y_send[pl.ds(8 * i, 8)] = o32[rows, :].reshape(8, 16, 128).astype(BF16)

    each(0, 8, pack)

    def send_conv(i):
        device, other = group(i)
        copy(y_send.at[other], y_recv.at[me], 6, device).start()

    others(64, send_conv)

    sum_bias(g32, m32, b_send)

    def send_bias(i):
        x2 = (x + i) % 4
        copy(b_send.at[x2], b_recv.at[x], 5, (s, 4 * z + x2)).start()

    others(4, send_bias)


    for hf in range(2):
        all_of(c_send.at[hf], c_recv.at[hf], 3 + hf, 3).wait()
        total = jnp.sum(c_recv[hf].astype(F32), axis=0) * filter_scale
        c_sum[:, 2 * hf : 2 * hf + 2, :] = total.reshape(16, 2, 128)
    c_mine[...] = regroup(c_sum[...].reshape(64, 128)).reshape(64, 1, 128)

    def send_cross(i):
        device, other = group(i)
        copy(c_mine.at[other], c_last.at[me], 7, device).start()

    others(64, send_cross)
    y_recv[me] = y_send[me]
    mine = [
        pltpu.make_async_copy(b_send.at[x], b_recv.at[x], loads.at[0]),
        pltpu.make_async_copy(c_mine.at[me], c_last.at[me], loads.at[1]),
        pltpu.make_async_copy(key_grad, key_out, loads.at[2]),
        pltpu.make_async_copy(value_grad, value_out, loads.at[3]),
    ]
    mine[0].start()
    mine[1].start()

    all_of(y_send, y_recv, 6, 63).wait()
    conv = from_tiles(y_recv)
    for jj in range(4):
        rows = slice(128 * jj, 128 * jj + 128)
        mixed_grad = conv[jj] + gain_in[...] * grad_in[rows, :].astype(F32)
        key_grad[rows, :] = (mixed_grad * value_in[rows, :].astype(F32)).astype(BF16)
        value_grad[rows, :] = (mixed_grad * key_in[rows, :].astype(F32)).astype(BF16)
    mine[2].start()
    mine[3].start()

    all_of(b_send, b_recv, 5, 3).wait()
    copy(c_last.at[pl.ds(0, 63)], c_last.at[pl.ds(0, 63)], 7, group(1)[0]).wait()
    for one in mine:
        one.wait()


def spread(parts):
    lane, row = iotas(64, 256)
    total = None
    for f in range(4):
        place = jnp.where(lane == 4 * row + f, 1.0, 0.0).astype(F32)
        moved = jnp.dot(
            parts[32 * f : 32 * f + 32, :], place, precision=lax.Precision.HIGHEST, preferred_element_type=F32
        )
        total = moved if total is None else total + moved
    return total


def finish(
    bias_scale,
    key_ref,
    value_ref,
    c_ref,
    b_ref,
    key_out,
    value_out,
    filter_out,
    bias_out,
    c_in,
    b_in,
    key_in,
    value_in,
    turned,
    bias_grad,
    loads,
    stores,
):
    loaded = [
        pltpu.make_async_copy(c_ref, c_in, loads.at[0]),
        pltpu.make_async_copy(b_ref, b_in, loads.at[1]),
        pltpu.make_async_copy(key_ref, key_in, loads.at[2]),
        pltpu.make_async_copy(value_ref, value_in, loads.at[3]),
    ]
    stored = [
        pltpu.make_async_copy(key_in, key_out, stores.at[0]),
        pltpu.make_async_copy(value_in, value_out, stores.at[1]),
        pltpu.make_async_copy(turned, filter_out, stores.at[2]),
        pltpu.make_async_copy(bias_grad, bias_out, stores.at[3]),
    ]
    for one in loaded:
        one.start()
    loaded[0].wait()
    turned[...] = spread(c_in[...].reshape(64, 128).T)
    stored[2].start()
    loaded[1].wait()
    sums = b_in[...]
    sub = lax.broadcasted_iota(jnp.int32, (8, 128), 0)
    sums = jnp.concatenate([jnp.where(sub < 4, sums[0], sums[1]), jnp.where(sub < 4, sums[2], sums[3])], axis=0)
    bias_grad[...] = jnp.sum(sums.T, axis=0, keepdims=True) * bias_scale
    stored[3].start()
    for load, store in zip(loaded[2:], stored):
        load.wait()
        store.start()
    for one in stored:
        one.wait()


def per_device(scales, key_proj, value_proj, grad_out, filter_taps, skip_gain):
    bias_scale, filter_scale = scales
    hbm = pl.BlockSpec(memory_space=pltpu.HBM)
    block = jax.ShapeDtypeStruct((512, 256), BF16)
    outs = pl.pallas_call(
        functools.partial(kernel, filter_scale),
        out_shape=(
            block,
            block,
            jax.ShapeDtypeStruct((64, 1, 128), F32),
            jax.ShapeDtypeStruct((4, 8, 128), F32),
        ),
        in_specs=[hbm] * 5,
        out_specs=(hbm,) * 4,
        scratch_shapes=[
            pltpu.VMEM((64, 16, 128), BF16),
            pltpu.VMEM((512, 256), BF16),
            pltpu.VMEM((512, 256), BF16),
            pltpu.VMEM((512, 256), BF16),
            pltpu.VMEM((512, 256), BF16),
            pltpu.VMEM((512, 256), BF16),
            pltpu.VMEM((512, 256), BF16),
            pltpu.VMEM((1, 256), F32),
            pltpu.VMEM((64, 16, 128), BF16),
            pltpu.VMEM((16, 16, 128), BF16),
            pltpu.VMEM((2, 64, 16, 128), BF16),
            pltpu.VMEM((2, 64, 16, 128), BF16),
            pltpu.VMEM((4, 8, 128), F32),
            pltpu.VMEM((64, 16, 128), BF16),
            pltpu.VMEM((4, 32, 128), F32),
            pltpu.VMEM((2, 4, 32, 128), BF16),
            pltpu.VMEM((2, 4, 32, 128), BF16),
            pltpu.VMEM((16, 4, 128), F32),
            pltpu.VMEM((64, 1, 128), F32),
            pltpu.VMEM((2, 544, 128), F32),
            pltpu.VMEM((2, 512, 128), F32),
            pltpu.VMEM((264, 128), F32),
            pltpu.VMEM((4, 256, 512), BF16),
            pltpu.VMEM((2, 640, 256), BF16),
            pltpu.VMEM((4, 8, 512, 256), BF16),
            pltpu.VMEM((256, 128), F32),
            pltpu.VMEM((1024, 128), F32),
            pltpu.VMEM((2, 384, 128), BF16),
            pltpu.VMEM((2, 256, 2048), BF16),
            pltpu.VMEM((2, 256, 512), F32),
            pltpu.SemaphoreType.DMA((5,)),
            pltpu.SemaphoreType.DMA((8,)),
            pltpu.SemaphoreType.DMA((8,)),
        ],
        name="hyena_exchange",
        compiler_params=pltpu.CompilerParams(
            collective_id=0, has_side_effects=True, vmem_limit_bytes=60 << 20
        ),
    )(key_proj, value_proj, grad_out, filter_taps, skip_gain.reshape(1, 256))
    key_grad, value_grad, filter_grad, bias_grad = pl.pallas_call(
        functools.partial(finish, bias_scale),
        out_shape=(
            block,
            block,
            jax.ShapeDtypeStruct((32, 256), F32),
            jax.ShapeDtypeStruct((1, 16), F32),
        ),
        in_specs=[hbm] * 4,
        out_specs=(hbm,) * 4,
        scratch_shapes=[
            pltpu.VMEM((64, 1, 128), F32),
            pltpu.VMEM((4, 8, 128), F32),
            pltpu.VMEM((512, 256), BF16),
            pltpu.VMEM((512, 256), BF16),
            pltpu.VMEM((32, 256), F32),
            pltpu.VMEM((1, 16), F32),
            pltpu.SemaphoreType.DMA((4,)),
            pltpu.SemaphoreType.DMA((4,)),
        ],
        name="hyena_finish",
        compiler_params=pltpu.CompilerParams(vmem_limit_bytes=60 << 20),
    )(*outs)
    return key_grad, value_grad, filter_grad, bias_grad.reshape(16)


def solution(mesh):
    in_specs = (P("seq", "chan"), P("seq", "chan"), P("seq", "chan"), P("seq", None), P("chan"))
    out_specs = (P("seq", "chan"), P("seq", "chan"), P(("seq", "chan"), None), P(("chan", "seq")))
    scales = (1.0 / math.sqrt(8192), 1.0 / math.sqrt(8192 * 16))
    return jax.shard_map(
        functools.partial(per_device, scales),
        mesh=mesh,
        in_specs=in_specs,
        out_specs=out_specs,
        check_vma=False,
    )
```

```python
import functools
import math

import jax
import jax.numpy as jnp
from jax import lax
from jax.experimental import pallas as pl
from jax.experimental.pallas import tpu as pltpu
from jax.sharding import PartitionSpec as P

MESH = pl.DeviceIdType.MESH
F32, BF16 = jnp.float32, jnp.bfloat16
NT = (((1,), (1,)), ((), ()))


def farthest_first(count):
    def ring(step):
        return min(step, 4 - step)

    def hops(i):
        if count == 4:
            return ring(i)
        x = i % 4 if count == 64 else 0
        rest = i // 4 if count == 64 else i
        return ring(rest // 4) + rest // 2 % 2 + ring(x)

    return sorted(range(1, count), key=hops, reverse=True)


def dot_nt(a, b):
    return lax.dot_general(a, b, NT, preferred_element_type=F32)


def iotas(rows, cols=128):
    lane = lax.broadcasted_iota(jnp.int32, (rows, cols), 1)
    return lane, lax.broadcasted_iota(jnp.int32, (rows, cols), 0)


def eye(size):
    lane, row = iotas(size, size)
    return jnp.where(lane == row, 1.0, 0.0).astype(BF16)


def halves(low, high):
    sub = lax.broadcasted_iota(jnp.int32, low.shape, 1)
    return jnp.where(sub < 4, low, high)


def turn(rows):
    return pltpu.roll(rows, 4, 1)


def to_tiles(block, tiles):
    flipped = dot_nt(eye(256), block).reshape(32, 8, 512)
    v = [flipped[:, :, 128 * jj : 128 * jj + 128] for jj in range(4)]
    even = jnp.concatenate([halves(v[0], turn(v[1])), halves(v[2], turn(v[3]))], axis=1)
    odd = jnp.concatenate([halves(turn(v[0]), v[1]), halves(turn(v[2]), v[3])], axis=1)
    tiles[...] = jnp.stack([even, odd], axis=1).reshape(64, 16, 128).astype(BF16)


def pair_rows(block):
    flipped = dot_nt(eye(256), block).reshape(32, 8, 512)
    sub = lax.broadcasted_iota(jnp.int32, (32, 8, 128), 1) // 2
    turned = [[pltpu.roll(flipped[:, :, 128 * jj : 128 * jj + 128], 2 * r, 1) if r else flipped[:, :, 128 * jj : 128 * jj + 128] for r in range(4)] for jj in range(4)]

    def merge(shift):
        rows = turned[0][-shift % 4]
        for jj in range(1, 4):
            rows = jnp.where(sub == jj, turned[jj][(jj - shift) % 4], rows)
        return rows

    return [[merge(2 * par + hf) for par in range(2)] for hf in range(2)]


def to_pair_tiles(grad, mixed, tiles):
    g, m = pair_rows(grad), pair_rows(mixed)
    for hf in range(2):
        both = [jnp.concatenate([g[hf][par], m[hf][par]], axis=1) for par in range(2)]
        tiles[hf] = jnp.stack(both, axis=1).reshape(64, 16, 128).astype(BF16)


def from_tiles(tiles):
    pairs = tiles[...].astype(F32).reshape(32, 32, 128)
    e0, e1, o0, o1 = (pairs[:, 8 * i : 8 * i + 8, :] for i in range(4))
    v = [halves(e0, turn(o0)), halves(turn(e0), o0), halves(e1, turn(o1)), halves(turn(e1), o1)]
    return [dot_nt(eye(128), one.reshape(256, 128).astype(BF16)) for one in v]


def unpack_taps(src, dst):
    lane, row = iotas(128)
    reverse = jnp.where(lane + row == 127, 1.0, 0.0).astype(BF16)
    dst[8:264, :] = jnp.dot(src[...].reshape(256, 128), reverse, preferred_element_type=F32)


def unpack_pairs(src, g32, m32):
    def one(i, c):
        rows = pl.ds(pl.multiple_of(128 * i, 128), 128)
        both = src[pl.ds(16 * i, 16)].astype(F32)
        g32[rows, :] = both[:, 0:8, :].reshape(128, 128)
        m32[rows, :] = both[:, 8:16, :].reshape(128, 128)
        return c

    lax.fori_loop(0, 4, one, 0)


def build_toeplitz(h32, f, t_ref, i):
    lane, row = iotas(128)
    mask = lane + row >= 127
    e, par = i // 2, i % 2
    rows = [h32[pl.ds(8 + 4 * (4 * i + j - 1) + f, 1), :] for j in range(5)]
    for d0 in range(4):
        before = jnp.broadcast_to(rows[d0], (128, 128))
        here = jnp.broadcast_to(rows[d0 + 1], (128, 128))
        t = pltpu.roll(jnp.where(mask, here, before), 1, 1, stride=1, stride_axis=0)
        t_ref[e, 128 * d0 : 128 * d0 + 128, 128 * par : 128 * par + 128] = t.astype(BF16)


def build_gcat(g32, f, gcat, gt5):
    jj = lax.broadcasted_iota(jnp.int32, (256, 128), 0) % 4
    unit = eye(128)
    for d0 in range(5):
        block = g32[pl.ds(f + 2 * (d0 if d0 < 4 else 16), 256, stride=2), :]
        if 0 < d0 < 4:
            later = g32[pl.ds(f + 2 * (d0 + 12), 256, stride=2), :]
            block = jnp.where(jj + d0 < 4, block, later)
        block = block.astype(BF16)
        if d0 < 4:
            gcat[:, 128 * d0 : 128 * d0 + 128] = block
        gt5[128 * d0 : 128 * d0 + 128, :] = dot_nt(unit, block).astype(BF16)


def convolve(gcat, t_ref, acc):
    acc[...] = jnp.zeros_like(acc)
    for e in range(8):
        n = 256 - 32 * e
        y = jnp.dot(gcat[32 * e : 256, :], t_ref[e], preferred_element_type=F32)
        acc[0:n, :] += y[:, 0:128]
        acc[0 : n - 16, :] += y[16:, 128:256]


def build_rt(m32, f, mpad, rt):
    mpad[128:384, :] = m32[pl.ds(f, 256, stride=2), :].astype(BF16)
    lane, row = iotas(128)
    flip = jnp.where(lane == (row // 16) * 16 + 15 - row % 16, 1.0, 0.0).astype(BF16)
    for d in range(8):
        t = dot_nt(flip, mpad[128 - 16 * d : 384 - 16 * d, :]).astype(BF16)
        for a in range(8):
            piece = t[16 * a : 16 * a + 16, :]
            rt[16 * d : 16 * d + 16, 256 * a : 256 * a + 256] = piece
            rt[128 + 16 * d : 144 + 16 * d, 256 * a + 128 : 256 * a + 256] = piece[:, 0:128]


def correlate(rt, gt5, out, beside):
    for half in range(2):
        acc = None
        for a in range(8):
            rows = gt5[16 * a + 256 * half : 16 * a + 256 * half + 256, :]
            y = dot_nt(rt[:, 256 * a : 256 * a + 256], rows)
            acc = y if acc is None else acc + y
            beside(8 * half + a)
        out[:, 256 * half : 256 * half + 256] = acc


def sum_diagonals(out, f2, c_ref):
    lane, row = iotas(16)
    mask = lane + row >= 15
    after = jnp.zeros((16, 128), F32)
    for d1 in reversed(range(16)):
        for d0 in reversed(range(4)):
            here = out[16 * d1 : 16 * d1 + 16, 128 * d0 : 128 * d0 + 128]
            z = pltpu.roll(jnp.where(mask, here, after), 113, 1, stride=1, stride_axis=0)
            after = here
            c_ref[d0, pl.ds(2 * d1 + f2, 1), :] = jnp.sum(z[0:8] + z[8:16], axis=0, keepdims=True)


def sum_bias(g32, m32, b_send):
    parts = []
    for hf in range(2):

        def one(i, sums):
            rows = pl.ds(pl.multiple_of(32 * i, 32), 32)
            return sums + g32[hf, rows, :] * m32[hf, rows, :]

        sums = lax.fori_loop(0, 16, one, jnp.zeros((32, 128), F32)).reshape(4, 8, 128)
        sums = sums + turn(sums)
        parts.append(sums + pltpu.roll(sums, 2, 1))
    sub = lax.broadcasted_iota(jnp.int32, (4, 8, 128), 1)
    b_send[...] = jnp.where(sub // 2 % 2 == 0, parts[0], parts[1])


def regroup(rows):
    lane, row = iotas(64)
    to = row % 4
    result = rows
    for step in range(1, 4):
        moved = jnp.where(to + step < 4, pltpu.roll(rows, 64 - step, 0), pltpu.roll(rows, 4 - step, 0))
        moved = pltpu.roll(moved, 32 * step, 1)
        result = jnp.where((lane // 32 - to + 4) % 4 == step, moved, result)
    return result


def kernel(
    filter_scale,
    key_ref,
    value_ref,
    grad_ref,
    taps_ref,
    gain_ref,
    key_out,
    value_out,
    c_last,
    b_recv,
    y_recv,
    key_grad,
    value_grad,
    key_in,
    value_in,
    grad_in,
    taps_in,
    gain_in,
    h_send,
    h_recv,
    x_send,
    x_recv,
    b_send,
    y_send,
    c_ref,
    c_send,
    c_recv,
    c_sum,
    c_mine,
    g32,
    m32,
    h32,
    gcat,
    gt5,
    t_ref,
    acc,
    o32,
    mpad,
    rt,
    out,
    loads,
    sends,
    recvs,
):
    s, k = lax.axis_index("seq"), lax.axis_index("chan")
    y, c = s // 4, s % 4
    z, x = k // 4, k % 4
    me = 4 * s + x

    def place(i):
        z_lo = 1 - c // 2 if i // 2 % 2 else c // 2
        core = 1 - c % 2 if i % 2 else c % 2
        return (y + i // 4) % 4 * 4 + z_lo * 2 + core

    def group(i):
        s2 = place(i // 4)
        x2 = (x + i % 4) % 4
        return (s2, 4 * z + x2), 4 * s2 + x2

    def row(i):
        s2 = place(i)
        return (s2, k), s2

    def column(i):
        z2 = (z + i) % 4
        return (s, 4 * z2 + x), z2

    def copy(src, dst, sem, device):
        return pltpu.make_async_remote_copy(
            src_ref=src,
            dst_ref=dst,
            send_sem=sends.at[sem],
            recv_sem=recvs.at[sem],
            device_id=device,
            device_id_type=MESH,
        )

    def all_of(src, dst, sem, count):
        return copy(src.at[pl.ds(0, count)], dst.at[pl.ds(0, count)], sem, group(1)[0])

    def each(lo, hi, body):
        lax.fori_loop(lo, hi, lambda i, none: (body(i), none)[1], 0)

    def others(count, body):
        for i in farthest_first(count):
            body(i)

    inputs = (
        (taps_ref, taps_in),
        (grad_ref, grad_in),
        (key_ref, key_in),
        (value_ref, value_in),
        (gain_ref, gain_in),
    )
    fetches = [pltpu.make_async_copy(src, dst, loads.at[i]) for i, (src, dst) in enumerate(inputs)]
    for fetch in fetches:
        fetch.start()

    barrier = pltpu.get_barrier_semaphore()

    def greet(device):
        pl.semaphore_signal(barrier, inc=1, device_id=device, device_id_type=MESH)

    others(64, lambda i: greet(group(i)[0]))
    others(4, lambda i: greet(column(i)[0]))

    fetches[0].wait()
    to_tiles(taps_in[...], h_send)
    for fetch in fetches[1:]:
        fetch.wait()
    mixed = (key_in[...].astype(F32) * value_in[...].astype(F32)).astype(BF16)
    to_pair_tiles(grad_in[...], mixed, x_send)

    h32[0:8, :] = jnp.zeros((8, 128), F32)
    for hf in range(2):
        g32[hf, 512:544, :] = jnp.zeros((32, 128), F32)
    for f2 in range(2):
        mpad[f2, 0:128, :] = jnp.zeros((128, 128), BF16)
    rt[...] = jnp.zeros_like(rt)

    pl.semaphore_wait(barrier, 66)

    def send_taps(i):
        device, s2 = row(i)
        copy(h_send.at[4 * s2 + x], h_recv.at[s], 0, device).start()

    def send_pairs(hf):
        def send(i):
            device, other = group(i)
            copy(x_send.at[hf, other], x_recv.at[hf, me], 1 + hf, device).start()

        return send

    others(16, send_taps)
    others(64, send_pairs(0))
    all_of(x_send.at[0], x_recv.at[0], 1, 63).wait_send()
    others(64, send_pairs(1))
    h_recv[s] = h_send[me]
    for hf in range(2):
        x_recv[hf, me] = x_send[hf, me]

    all_of(h_send, h_recv, 0, 15).wait()
    unpack_taps(h_recv, h32)

    for hf in range(2):
        pair = all_of(x_send.at[hf], x_recv.at[hf], 1 + hf, 63)
        pair.wait_recv()
        if hf == 1:
            pair.wait_send()
        unpack_pairs(x_recv.at[hf], g32.at[hf], m32.at[hf])

        for f2 in range(2):
            f = 2 * hf + f2
            build_gcat(g32.at[hf], f2, gcat.at[f], gt5.at[f2])
            build_rt(m32.at[hf], f2, mpad.at[f2], rt.at[f2])
            correlate(rt.at[f2], gt5.at[f2], out.at[f2], functools.partial(build_toeplitz, h32, f, t_ref.at[f]))
            sum_diagonals(out.at[f2], f2, c_ref)

        c_send[hf] = c_ref[...].astype(BF16)

        def send_part(i):
            device, z2 = column(i)
            copy(c_send.at[hf, z2], c_recv.at[hf, z], 3 + hf, device).start()

        others(4, send_part)
        c_recv[hf, z] = c_send[hf, z]

    for f in range(4):
        convolve(gcat.at[f], t_ref.at[f], acc.at[f])
        o32[pl.ds(f, 256, stride=4), :] = acc[f]

    def pack(i):
        rows = pl.ds(pl.multiple_of(128 * i, 8), 128)
        y_send[pl.ds(8 * i, 8)] = o32[rows, :].reshape(8, 16, 128).astype(BF16)

    each(0, 8, pack)

    def send_conv(i):
        device, other = group(i)
        copy(y_send.at[other], y_recv.at[me], 6, device).start()

    others(64, send_conv)

    sum_bias(g32, m32, b_send)

    def send_bias(i):
        x2 = (x + i) % 4
        copy(b_send.at[x2], b_recv.at[x], 5, (s, 4 * z + x2)).start()

    others(4, send_bias)


    for hf in range(2):
        all_of(c_send.at[hf], c_recv.at[hf], 3 + hf, 3).wait()
        total = jnp.sum(c_recv[hf].astype(F32), axis=0) * filter_scale
        c_sum[:, 2 * hf : 2 * hf + 2, :] = total.reshape(16, 2, 128)
    c_mine[...] = regroup(c_sum[...].reshape(64, 128)).reshape(64, 1, 128)

    def send_cross(i):
        device, other = group(i)
        copy(c_mine.at[other], c_last.at[me], 7, device).start()

    others(64, send_cross)
    y_recv[me] = y_send[me]
    mine = [
        pltpu.make_async_copy(b_send.at[x], b_recv.at[x], loads.at[0]),
        pltpu.make_async_copy(c_mine.at[me], c_last.at[me], loads.at[1]),
        pltpu.make_async_copy(key_grad, key_out, loads.at[2]),
        pltpu.make_async_copy(value_grad, value_out, loads.at[3]),
    ]
    mine[0].start()
    mine[1].start()

    all_of(y_send, y_recv, 6, 63).wait()
    conv = from_tiles(y_recv)
    for jj in range(4):
        rows = slice(128 * jj, 128 * jj + 128)
        mixed_grad = conv[jj] + gain_in[...] * grad_in[rows, :].astype(F32)
        key_grad[rows, :] = (mixed_grad * value_in[rows, :].astype(F32)).astype(BF16)
        value_grad[rows, :] = (mixed_grad * key_in[rows, :].astype(F32)).astype(BF16)
    mine[2].start()
    mine[3].start()

    all_of(b_send, b_recv, 5, 3).wait()
    copy(c_last.at[pl.ds(0, 63)], c_last.at[pl.ds(0, 63)], 7, group(1)[0]).wait()
    for one in mine:
        one.wait()


def spread(parts):
    high = parts.astype(BF16)
    rest = parts - high.astype(F32)
    middle = rest.astype(BF16)
    low = (rest - middle.astype(F32)).astype(BF16)
    lane, row = iotas(64, 256)
    total = jnp.zeros((96, 256), F32)
    for f in range(4):
        rows = slice(32 * f, 32 * f + 32)
        terms = jnp.concatenate([high[rows], middle[rows], low[rows]], axis=0)
        place = jnp.where(lane == 4 * row + f, 1.0, 0.0).astype(BF16)
        total = total + jnp.dot(terms, place, preferred_element_type=F32)
    return (total[64:96] + total[32:64]) + total[0:32]


def finish(
    bias_scale,
    key_ref,
    value_ref,
    c_ref,
    b_ref,
    key_out,
    value_out,
    filter_out,
    bias_out,
    c_in,
    b_in,
    key_in,
    value_in,
    turned,
    bias_grad,
    loads,
    stores,
):
    loaded = [
        pltpu.make_async_copy(c_ref, c_in, loads.at[0]),
        pltpu.make_async_copy(b_ref, b_in, loads.at[1]),
        pltpu.make_async_copy(key_ref, key_in, loads.at[2]),
        pltpu.make_async_copy(value_ref, value_in, loads.at[3]),
    ]
    stored = [
        pltpu.make_async_copy(key_in, key_out, stores.at[0]),
        pltpu.make_async_copy(value_in, value_out, stores.at[1]),
        pltpu.make_async_copy(turned, filter_out, stores.at[2]),
        pltpu.make_async_copy(bias_grad, bias_out, stores.at[3]),
    ]
    for one in loaded:
        one.start()
    loaded[0].wait()
    turned[...] = spread(c_in[...].reshape(64, 128).T)
    stored[2].start()
    loaded[1].wait()
    sums = b_in[...]
    sub = lax.broadcasted_iota(jnp.int32, (8, 128), 0)
    sums = jnp.concatenate([jnp.where(sub < 4, sums[0], sums[1]), jnp.where(sub < 4, sums[2], sums[3])], axis=0)
    bias_grad[...] = jnp.sum(sums.T, axis=0, keepdims=True) * bias_scale
    stored[3].start()
    for load, store in zip(loaded[2:], stored):
        load.wait()
        store.start()
    for one in stored:
        one.wait()


def per_device(scales, key_proj, value_proj, grad_out, filter_taps, skip_gain):
    bias_scale, filter_scale = scales
    hbm = pl.BlockSpec(memory_space=pltpu.HBM)
    block = jax.ShapeDtypeStruct((512, 256), BF16)
    outs = pl.pallas_call(
        functools.partial(kernel, filter_scale),
        out_shape=(
            block,
            block,
            jax.ShapeDtypeStruct((64, 1, 128), F32),
            jax.ShapeDtypeStruct((4, 8, 128), F32),
        ),
        in_specs=[hbm] * 5,
        out_specs=(hbm,) * 4,
        scratch_shapes=[
            pltpu.VMEM((64, 16, 128), BF16),
            pltpu.VMEM((512, 256), BF16),
            pltpu.VMEM((512, 256), BF16),
            pltpu.VMEM((512, 256), BF16),
            pltpu.VMEM((512, 256), BF16),
            pltpu.VMEM((512, 256), BF16),
            pltpu.VMEM((512, 256), BF16),
            pltpu.VMEM((1, 256), F32),
            pltpu.VMEM((64, 16, 128), BF16),
            pltpu.VMEM((16, 16, 128), BF16),
            pltpu.VMEM((2, 64, 16, 128), BF16),
            pltpu.VMEM((2, 64, 16, 128), BF16),
            pltpu.VMEM((4, 8, 128), F32),
            pltpu.VMEM((64, 16, 128), BF16),
            pltpu.VMEM((4, 32, 128), F32),
            pltpu.VMEM((2, 4, 32, 128), BF16),
            pltpu.VMEM((2, 4, 32, 128), BF16),
            pltpu.VMEM((16, 4, 128), F32),
            pltpu.VMEM((64, 1, 128), F32),
            pltpu.VMEM((2, 544, 128), F32),
            pltpu.VMEM((2, 512, 128), F32),
            pltpu.VMEM((264, 128), F32),
            pltpu.VMEM((4, 256, 512), BF16),
            pltpu.VMEM((2, 640, 256), BF16),
            pltpu.VMEM((4, 8, 512, 256), BF16),
            pltpu.VMEM((4, 256, 128), F32),
            pltpu.VMEM((1024, 128), F32),
            pltpu.VMEM((2, 384, 128), BF16),
            pltpu.VMEM((2, 256, 2048), BF16),
            pltpu.VMEM((2, 256, 512), F32),
            pltpu.SemaphoreType.DMA((5,)),
            pltpu.SemaphoreType.DMA((8,)),
            pltpu.SemaphoreType.DMA((8,)),
        ],
        name="hyena_exchange",
        compiler_params=pltpu.CompilerParams(
            collective_id=0, has_side_effects=True, vmem_limit_bytes=60 << 20
        ),
    )(key_proj, value_proj, grad_out, filter_taps, skip_gain.reshape(1, 256))
    key_grad, value_grad, filter_grad, bias_grad = pl.pallas_call(
        functools.partial(finish, bias_scale),
        out_shape=(
            block,
            block,
            jax.ShapeDtypeStruct((32, 256), F32),
            jax.ShapeDtypeStruct((1, 16), F32),
        ),
        in_specs=[hbm] * 4,
        out_specs=(hbm,) * 4,
        scratch_shapes=[
            pltpu.VMEM((64, 1, 128), F32),
            pltpu.VMEM((4, 8, 128), F32),
            pltpu.VMEM((512, 256), BF16),
            pltpu.VMEM((512, 256), BF16),
            pltpu.VMEM((32, 256), F32),
            pltpu.VMEM((1, 16), F32),
            pltpu.SemaphoreType.DMA((4,)),
            pltpu.SemaphoreType.DMA((4,)),
        ],
        name="hyena_finish",
        compiler_params=pltpu.CompilerParams(vmem_limit_bytes=60 << 20),
    )(*outs)
    return key_grad, value_grad, filter_grad, bias_grad.reshape(16)


def solution(mesh):
    in_specs = (P("seq", "chan"), P("seq", "chan"), P("seq", "chan"), P("seq", None), P("chan"))
    out_specs = (P("seq", "chan"), P("seq", "chan"), P(("seq", "chan"), None), P(("chan", "seq")))
    scales = (1.0 / math.sqrt(8192), 1.0 / math.sqrt(8192 * 16))
    return jax.shard_map(
        functools.partial(per_device, scales),
        mesh=mesh,
        in_specs=in_specs,
        out_specs=out_specs,
        check_vma=False,
    )
```
